256 devices in a mesh: dp: 8 (over y, core), ctx: 32 (over z, x).
Axes of the slice: x: 4, y: 4, z: 8, core: 2. Of those that a mesh axis runs over, the one named last changes fastest.
Arguments:
- doc_lengths: int32 [8, 8], P('dp'), may hold values from 1 to 2048, 4096 in all within a row
- values: bfloat16 [8, 4096, 4096], P('dp', 'ctx'), may hold values from -6 to 6
- gate_short: bfloat16 [8, 4096, 4096], P('dp', 'ctx'), may hold values from -6 to 6
- gate_long: bfloat16 [8, 4096, 4096], P('dp', 'ctx'), may hold values from -6 to 6
- short_taps: float32 [7, 4096], replicated, may hold values from -2 to 2
- long_taps: float32 [128, 4096], replicated
- cotangent: bfloat16 [8, 4096, 4096], P('dp', 'ctx'), may hold values from -6 to 6
Outputs:
- output: bfloat16 [8, 4096, 4096], P('dp', 'ctx')
- grad_gate_short: bfloat16 [8, 4096, 4096], P('dp', 'ctx')
- grad_values: bfloat16 [8, 4096, 4096], P('dp', 'ctx')
- grad_gate_long: bfloat16 [8, 4096, 4096], P('dp', 'ctx')
- grad_short_taps: float32 [7, 4096], replicated
- grad_long_taps: float32 [128, 4096], replicated
The draws below stay inside these ranges and needn't reach their ends.
Inputs may be any that keep to these rules, and one draw needn't show every extreme that they name: `doc_lengths`: each row holds the lengths of the 8 documents of one context in order; they sum to 4096, and the longest is exactly 2048.
All inputs are finite; a program needn't handle non-finite values.
Results may differ from the reference program's by a relative error of at most 0.0065.
Values may be sent and summed in bfloat16 or wider, within the bound.
No kernel may reach another device: no remote copies, remote signals or barrier semaphores. Data moves between devices by JAX's collectives and lax.ppermute only.
A program may use at most 256 MiB of HBM per device.

```python
import math
import jax
import jax.numpy as jnp
import numpy as np
from jax import lax

D = 4096
TAPS_SE = 7
TAPS_MR = 128
NDOC = 8
CTXLEN = 4096
DOC_MOST = 2048
N_DP = 8


def draw_long_taps(key, part):
    key = jax.random.fold_in(key, 7)
    decay_key, noise_key = jax.random.split(key)
    decay_len = jnp.exp(jax.random.uniform(decay_key, (D,), jnp.float32, jnp.log(10.0), jnp.log(1000.0)))
    noise_part = jax.random.normal(noise_key, (TAPS_MR, D), jnp.float32)
    ratio_step = jnp.exp(-1.0 / decay_len)
    lag_index = jnp.arange(TAPS_MR, dtype=jnp.float32)
    energy = (1.0 - ratio_step ** (2.0 * TAPS_MR)) / (1.0 - ratio_step ** 2)
    return noise_part * ratio_step[None, :] ** lag_index[:, None] / jnp.sqrt(energy)[None, :]


def levels(own_key, dims, shards, smallest, high):
    factor_of = 1.0
    for axis_at, parts in shards:
        heights = jax.random.uniform(jax.random.fold_in(jax.random.fold_in(own_key, 6), axis_at), (parts,), jnp.float32, smallest / len(shards), high / len(shards))
        factor_of = factor_of * jnp.repeat(jnp.exp(heights), dims[axis_at] // parts).reshape((-1,) + (1,) * (len(dims) - 1 - axis_at))
    return factor_of


def profile(number_of, total, limit, skew):
    loads = [(1 << 20) // math.isqrt(grade ** skew) + 1 for grade in range(2, number_of + 1)]
    surplus, counts = total - limit - (number_of - 1), [1] * (number_of - 1)
    while surplus > 0:
        free = [i for i in range(number_of - 1) if counts[i] < limit]
        mass, budget = sum([loads[i] for i in free]), surplus
        for i in free:
            addition = min(limit - counts[i], max(1, budget * loads[i] // mass), surplus)
            counts[i] = counts[i] + addition
            surplus = surplus - addition
    return np.array([limit] + counts)


def ragged(own_key, count, total, limit, skew):
    if count == 2:
        one = jax.random.randint(own_key, (), max(1, total - limit), min(limit, total - 1) + 1)
        return jnp.stack([one, total - one])
    sizes = jnp.asarray(profile(count, total, limit, skew), jnp.int32)
    couples = (count - 1) // 2
    giver, taker = sizes[1:1 + 2 * couples:2], sizes[2:2 + 2 * couples:2]
    slack = jnp.minimum(giver - 1, limit - taker)
    shifted = jax.random.randint(jax.random.fold_in(own_key, 1), (couples,), 0, 1 << 20) % (slack + 1)
    sizes = sizes.at[1:1 + 2 * couples:2].set(giver - shifted).at[2:2 + 2 * couples:2].set(taker + shifted)
    return sizes[jax.random.permutation(jax.random.fold_in(own_key, 2), count)]


def gaussian(rng, dims, scale, bound, pieces=(), kind=jnp.bfloat16):
    drawn = jax.random.normal(rng, dims, jnp.float32) * scale
    if len(pieces) > 0:
        drawn = levels(rng, dims, pieces, -0.22, 0.18) * drawn
    return jnp.clip(drawn, min=-bound, max=bound).astype(kind)


def setup_inputs(seed: int = 0) -> dict:
    keys = jax.random.split(jax.random.key(seed), 8)
    doc_lengths = jax.vmap(lambda own: ragged(own, NDOC, CTXLEN, DOC_MOST, 2))(jax.random.split(keys[0], N_DP)).reshape((N_DP, NDOC)).astype(jnp.int32)
    values = gaussian(keys[1], (N_DP, CTXLEN, D), 1.0, 6.0, ((0, 8), (1, 32)))
    gate_short = gaussian(keys[2], (N_DP, CTXLEN, D), 1.0, 6.0, ((0, 8), (1, 32)))
    gate_long = gaussian(keys[3], (N_DP, CTXLEN, D), 1.0, 6.0, ((0, 8), (1, 32)))
    short_taps = gaussian(keys[4], (TAPS_SE, D), TAPS_SE ** -0.5, 2.0, (), jnp.float32)
    long_taps = draw_long_taps(jax.random.fold_in(keys[7], 71), 0)
    cotangent = gaussian(keys[6], (N_DP, CTXLEN, D), 1.0, 6.0, ((0, 8), (1, 32)))
    return {"doc_lengths": doc_lengths, "values": values, "gate_short": gate_short, "gate_long": gate_long, "short_taps": short_taps, "long_taps": long_taps, "cotangent": cotangent}


def reach_of(lengths, positions):
    lengths = lengths.astype(jnp.int32)
    starts = (jnp.cumsum(lengths) - lengths).astype(jnp.int32)
    before = jnp.where(starts[None, :] <= positions[:, None], starts[None, :], 0)
    return (positions - lax.optimization_barrier(jnp.max(before, axis=1))).astype(jnp.int32)

def forward_filter(signal, filter_taps, reach):
    tap_count = filter_taps.shape[0]
    length = signal.shape[0]
    padded = jnp.pad(signal, ((tap_count - 1, 0), (0, 0)))

    def add_tap(offset, summed):
        offset = jnp.asarray(offset).astype(jnp.int32)
        window = lax.dynamic_slice_in_dim(padded, (tap_count - 1 - offset).astype(jnp.int32), length, 0).astype(jnp.float32)
        weight = lax.dynamic_index_in_dim(filter_taps, offset, 0, keepdims=False)
        return summed + weight[None, :] * jnp.where((reach >= offset)[:, None], window, jnp.zeros_like(window))
    return lax.fori_loop(0, tap_count, add_tap, jnp.zeros((length, signal.shape[1]), jnp.float32))

def adjoint_filter(adjoint, filter_taps, reach):
    tap_count = filter_taps.shape[0]
    length = adjoint.shape[0]
    padded = jnp.pad(adjoint, ((0, tap_count - 1), (0, 0)))
    reach_pad = jnp.pad(reach, (0, tap_count - 1))

    def add_tap(offset, summed):
        offset = jnp.asarray(offset).astype(jnp.int32)
        window = lax.dynamic_slice_in_dim(padded, offset, length, 0).astype(jnp.float32)
        masked = lax.dynamic_slice_in_dim(reach_pad, offset, length, 0) >= offset
        weight = lax.dynamic_index_in_dim(filter_taps, offset, 0, keepdims=False)
        return summed + weight[None, :] * jnp.where(masked[:, None], window, jnp.zeros_like(window))
    return lax.fori_loop(0, tap_count, add_tap, jnp.zeros((length, adjoint.shape[1]), jnp.float32))

def filter_grad(adjoint, signal, reach, tap_count):
    length = signal.shape[0]
    padded = jnp.pad(signal, ((tap_count - 1, 0), (0, 0)))
    weights = adjoint.astype(jnp.float32)

    def one_tap(offset):
        window = lax.dynamic_slice_in_dim(padded, (tap_count - 1 - offset).astype(jnp.int32), length, 0).astype(jnp.float32)
        product = weights * window
        return lax.optimization_barrier(jnp.sum(jnp.where((reach >= offset)[:, None], product, jnp.zeros_like(product)), axis=0))
    return lax.map(one_tap, jnp.arange(tap_count, dtype=jnp.int32))

def reference(doc_lengths, values, gate_short, gate_long, short_taps, long_taps, cotangent):

    def one_context(context_items):
        lengths, signal, gate_one, gate_two, upstream = context_items
        positions = jnp.arange(CTXLEN, dtype=jnp.int32)
        reach = reach_of(lengths, positions)
        short_mix = forward_filter(signal, short_taps, reach)
        mixed_short = (gate_one.astype(jnp.float32) * short_mix).astype(jnp.bfloat16)
        long_mix = forward_filter(mixed_short, long_taps, reach)
        output = (gate_two.astype(jnp.float32) * long_mix).astype(jnp.bfloat16)
        grad_gate_long = (upstream.astype(jnp.float32) * long_mix).astype(jnp.bfloat16)
        adj_long = (upstream.astype(jnp.float32) * gate_two.astype(jnp.float32)).astype(jnp.bfloat16)
        back_long = adjoint_filter(adj_long, long_taps, reach)
        long_terms = filter_grad(adj_long, mixed_short, reach, TAPS_MR)
        grad_gate_short = (back_long * short_mix).astype(jnp.bfloat16)
        adj_short = (back_long * gate_one.astype(jnp.float32)).astype(jnp.bfloat16)
        grad_values = adjoint_filter(adj_short, short_taps, reach).astype(jnp.bfloat16)
        short_terms = filter_grad(adj_short, signal, reach, TAPS_SE)
        return (output, grad_gate_short, grad_values, grad_gate_long, short_terms, long_terms)
    results = lax.map(one_context, (doc_lengths, values, gate_short, gate_long, cotangent))
    factor = 1.0 / math.sqrt(N_DP * CTXLEN)
    grad_short_taps = lax.optimization_barrier(jnp.sum(results[4], axis=0)) * factor
    grad_long_taps = lax.optimization_barrier(jnp.sum(results[5], axis=0)) * factor
    return (results[0], results[1], results[2], results[3], grad_short_taps, grad_long_taps)
```

```python
import math

import jax
import jax.numpy as jnp
import numpy as np
from jax import lax
from jax.experimental import pallas as pl
from jax.experimental.pallas import tpu as pltpu
from jax.sharding import PartitionSpec as P

BF = jnp.bfloat16
F32 = jnp.float32
LANES = 128


def halves(matrix):
    high = matrix.astype(np.float32).astype(BF)
    low = (matrix - high.astype(np.float64)).astype(np.float32).astype(BF)
    return high, low


def spectra(rows):
    points = 2 * rows
    theta = np.pi * (2 * np.arange(rows) + 1) / points
    angles = theta[:, None] * np.arange(points)[None, :]
    forward = np.concatenate([np.cos(angles), -np.sin(angles)], axis=0)
    inverse = forward.T / rows

    def pack(matrix):
        return np.concatenate(halves(matrix), axis=1)

    first = pack(forward[:, :rows])
    second = pack(forward[:, rows:])
    to_later = pack(inverse[rows:])
    to_first = pack(inverse[:rows])
    to_taps = pack(inverse[rows - np.arange(rows)])
    return first, second, to_later, to_first, to_taps


def passed_along(block, distance):
    devices = range(lax.axis_size("ctx"))
    route = [(i - distance, i) for i in devices if i - distance in devices]
    return lax.ppermute(block, "ctx", route)


def wide(row_mask, columns):
    return jnp.concatenate([row_mask] * (columns // LANES), axis=1)


def mix_kernel(reach_ref, v_ref, before_ref, gs_ref, gl_ref, up_ref, taps_ref,
               mixed_ref, adj_ref, short_ref, ext):
    rows, columns = v_ref.shape
    count = taps_ref.shape[0]
    ext[0:8, :] = before_ref[...].astype(F32)
    ext[8:, :] = v_ref[...].astype(F32)
    reach = wide(reach_ref[...], columns)
    total = taps_ref[0:1, :] * ext[8:, :]
    for j in range(1, count):
        window = ext[8 - j : 8 - j + rows, :]
        total = total + taps_ref[j : j + 1, :] * jnp.where(reach >= j, window, 0.0)
    short_ref[...] = total
    mixed_ref[...] = (gs_ref[...].astype(F32) * total).astype(BF)
    adj_ref[...] = (up_ref[...].astype(F32) * gl_ref[...].astype(F32)).astype(BF)


def times(left, right, conjugate_left):
    half = left.shape[0] // 2
    a, b = left[:half], left[half:]
    c, d = right[:half], right[half:]
    if conjugate_left:
        return jnp.concatenate([a * c + b * d, a * d - b * c], axis=0)
    return jnp.concatenate([a * c - b * d, a * d + b * c], axis=0)


def dot(matrix, data):
    return jnp.dot(matrix, data, preferred_element_type=F32)


def doubled(data):
    return jnp.concatenate([data, data], axis=0)


def main_kernel(meta_ref, reach_ref, left_ref, v_ref, before_ref, gs_ref, gl_ref, up_ref,
                mixed_ref, adj_ref, short_ref, prev_ref, next_ref, staps_ref, ltaps_ref,
                first_ref, second_ref, later_ref, front_ref, totaps_ref,
                out_ref, ggs_ref, gv_ref, ggl_ref, grads_ref, head_ref, tail_ref,
                long_acc, back_acc, spec_acc, taps_spec, ext, adj_ext):
    rows, columns = v_ref.shape
    count = staps_ref.shape[0]
    taps_spec[...] = dot(first_ref[...], doubled(ltaps_ref[...].astype(BF)))
    long_acc[...] = jnp.zeros_like(long_acc)
    back_acc[...] = jnp.zeros_like(back_acc)
    spec_acc[...] = jnp.zeros_like(spec_acc)
    at = lax.broadcasted_iota(jnp.int32, (rows, LANES), 0)

    def document(d, carry):
        begin = meta_ref[2 + d]
        end = meta_ref[3 + d]

        def inside(positions):
            return jnp.where((positions >= begin) & (positions < end), 1.0, 0.0)

        own = wide(inside(at), columns)
        own_bf = own.astype(BF)
        prev = prev_ref[...] * wide(inside(at - rows), columns).astype(BF)
        following = next_ref[...] * wide(inside(at + rows), columns).astype(BF)
        mixed = mixed_ref[...] * own_bf
        adj = adj_ref[...] * own_bf
        x_spec = dot(first_ref[...], doubled(prev)) + dot(second_ref[...], doubled(mixed))
        product = times(taps_spec[...], x_spec, False).astype(BF)
        long_acc[...] += own * dot(later_ref[...], doubled(product))
        a_spec = dot(first_ref[...], doubled(adj))
        spec_acc[...] += times(a_spec, x_spec, True)
        a_spec = a_spec + dot(second_ref[...], doubled(following))
        product = times(taps_spec[...], a_spec, True).astype(BF)
        back_acc[...] += own * dot(front_ref[...], doubled(product))
        return carry

    lax.fori_loop(meta_ref[0], meta_ref[1] + 1, document, 0)
    grads_ref[0:rows, :] = dot(totaps_ref[...], doubled(spec_acc[...].astype(BF))).astype(BF)

    long_mix = long_acc[...]
    out_ref[...] = (gl_ref[...].astype(F32) * long_mix).astype(BF)
    ggl_ref[...] = (up_ref[...].astype(F32) * long_mix).astype(BF)
    back = back_acc[...]
    ggs_ref[...] = (back * short_ref[...]).astype(BF)
    adj_short = (back * gs_ref[...].astype(F32)).astype(BF).astype(F32)
    head_ref[...] = adj_short[0:8].astype(BF)
    adj_ext[0:rows, :] = adj_short
    adj_ext[rows:, :] = jnp.zeros((8, columns), F32)
    ext[0:8, :] = before_ref[...].astype(F32)
    ext[8:, :] = v_ref[...].astype(F32)
    reach = wide(reach_ref[...], columns)
    left = wide(left_ref[...], columns)
    total = staps_ref[0:1, :] * adj_short
    terms = [jnp.sum(adj_short * ext[8:, :], axis=0, keepdims=True)]
    for j in range(1, count):
        total = total + staps_ref[j : j + 1, :] * jnp.where(
            left > j, adj_ext[j : j + rows, :], 0.0)
        window = ext[8 - j : 8 - j + rows, :]
        terms.append(jnp.sum(jnp.where(reach >= j, adj_short * window, 0.0), axis=0, keepdims=True))
    gv_ref[...] = total.astype(BF)
    tail_ref[...] = total[rows - 16 :]
    terms.append(jnp.zeros((8 - count, columns), F32))
    stacked = jnp.concatenate(terms, axis=0)
    grads_ref[rows:, :] = jnp.concatenate([stacked, jnp.zeros_like(stacked)], axis=0).astype(BF)


def on_device(doc_lengths, values, gate_short, gate_long, short_taps, long_taps, cotangent):
    v, gs, gl, up = values[0], gate_short[0], gate_long[0], cotangent[0]
    rows, channels = v.shape
    dp, ctx = lax.axis_size("dp"), lax.axis_size("ctx")
    columns = channels // dp
    lengths = doc_lengths[0]
    documents = lengths.shape[0]
    count = short_taps.shape[0]
    first_row = lax.axis_index("ctx") * rows
    ends = jnp.cumsum(lengths)
    bounds = jnp.concatenate([jnp.zeros((1,), jnp.int32), ends]) - first_row
    at = jnp.arange(rows, dtype=jnp.int32)
    low = jnp.sum((bounds[:documents] <= 0).astype(jnp.int32)) - 1
    high = jnp.sum((bounds[:documents] <= rows - 1).astype(jnp.int32)) - 1
    meta = jnp.concatenate([low[None], high[None], bounds])
    start_at = jnp.max(jnp.where(bounds[None, :documents] <= at[:, None], bounds[None, :documents],
                                 -first_row), axis=1)
    end_at = jnp.min(jnp.where(bounds[None, 1:] > at[:, None], bounds[None, 1:],
                               bounds[documents]), axis=1)
    reach = jnp.broadcast_to((at - start_at)[:, None], (rows, LANES))
    left = jnp.broadcast_to((end_at - at)[:, None], (rows, LANES))

    before = passed_along(v[rows - 8 :], 1)

    whole = lambda r: pl.BlockSpec((r, LANES), lambda i: (0, 0))
    block = lambda r: pl.BlockSpec((r, columns), lambda i: (0, i))
    params = pltpu.CompilerParams(vmem_limit_bytes=48 << 20)
    shaped = lambda r, t: jax.ShapeDtypeStruct((r, channels), t)
    mixed, adj, short = pl.pallas_call(
        mix_kernel,
        grid=(dp,),
        in_specs=[whole(rows), block(rows), block(8), block(rows), block(rows), block(rows), block(count)],
        out_specs=[block(rows)] * 3,
        out_shape=[shaped(rows, BF), shaped(rows, BF), shaped(rows, F32)],
        scratch_shapes=[pltpu.VMEM((rows + 8, columns), F32)],
        compiler_params=params,
    )(reach, v, before, gs, gl, up, short_taps)

    prev = passed_along(mixed, 1)
    following = passed_along(adj, -1)

    matrices = [jnp.asarray(m) for m in spectra(rows)]
    full = lambda m: pl.BlockSpec(m.shape, lambda i: (0, 0))
    out, ggs, gv, ggl, grads, head, tail = pl.pallas_call(
        main_kernel,
        grid=(dp,),
        in_specs=[pl.BlockSpec(memory_space=pltpu.SMEM), whole(rows), whole(rows), block(rows), block(8)]
        + [block(rows)] * 8 + [block(count), block(rows)] + [full(m) for m in matrices],
        out_specs=[block(rows)] * 4
        + [pl.BlockSpec((None, rows + 16, columns), lambda i: (i, 0, 0)), block(8), block(16)],
        out_shape=[shaped(rows, BF)] * 4
        + [jax.ShapeDtypeStruct((dp, rows + 16, columns), BF), shaped(8, BF), shaped(16, F32)],
        scratch_shapes=[
            pltpu.VMEM((rows, columns), F32), pltpu.VMEM((rows, columns), F32),
            pltpu.VMEM((2 * rows, columns), F32), pltpu.VMEM((2 * rows, columns), F32),
            pltpu.VMEM((rows + 8, columns), F32), pltpu.VMEM((rows + 8, columns), F32),
        ],
        compiler_params=params,
    )(meta, reach, left, v, before, gs, gl, up, mixed, adj, short, prev, following,
      short_taps, long_taps, *matrices)

    after = passed_along(head, -1).astype(F32)
    padded = jnp.concatenate([jnp.zeros((16, channels), F32), after, jnp.zeros((8, channels), F32)])
    for j in range(1, count):
        tail = tail + short_taps[j][None, :] * jnp.where(
            (left[rows - 16 :, :1] > j), padded[j : j + 16], 0.0)
    gv = lax.dynamic_update_slice(gv, tail.astype(BF), (rows - 16, 0))

    kept = rows + 8
    factor = 1.0 / math.sqrt(dp * ctx * rows)
    share = lax.all_to_all(grads[:, :kept], "dp", 0, 0, tiled=True)
    share = jnp.sum(share.astype(F32), axis=0).astype(BF)
    share = lax.all_to_all(share.reshape(ctx, -1, LANES), "ctx", 0, 0, tiled=True)
    share = (jnp.sum(share.astype(F32), axis=0) * factor).astype(BF)
    share = lax.all_to_all(jnp.broadcast_to(share[None], (ctx,) + share.shape), "ctx", 0, 0, tiled=True)
    share = share.reshape(1, kept, columns)
    share = lax.all_to_all(jnp.broadcast_to(share, (dp, kept, columns)), "dp", 0, 0, tiled=True)
    total = share.transpose(1, 0, 2).reshape(kept, channels).astype(F32)
    return (out[None], ggs[None], gv[None], ggl[None], total[rows : rows + count], total[:rows])


def solution(mesh):
    rowed = P("dp", "ctx", None)
    return jax.shard_map(
        on_device,
        mesh=mesh,
        in_specs=(P("dp", None), rowed, rowed, rowed, P(), P(), rowed),
        out_specs=(rowed, rowed, rowed, rowed, P(), P()),
        check_vma=False,
    )
```

```python
import math

import jax
import jax.numpy as jnp
import numpy as np
from jax import lax
from jax.experimental import pallas as pl
from jax.experimental.pallas import tpu as pltpu
from jax.sharding import PartitionSpec as P

BF = jnp.bfloat16
F32 = jnp.float32
LANES = 128
RIM = 8
CTX = ("z", "x")


def halves(matrix):
    high = matrix.astype(np.float32).astype(BF)
    low = (matrix - high.astype(np.float64)).astype(np.float32).astype(BF)
    return high, low


def spectra(rows):
    points = 2 * rows
    theta = np.pi * (2 * np.arange(rows) + 1) / points
    angles = theta[:, None] * np.arange(points)[None, :]
    forward = np.concatenate([np.cos(angles), -np.sin(angles)], axis=0)
    inverse = forward.T / rows

    def pack(matrix):
        return np.concatenate(halves(matrix), axis=1)

    def stack(matrix):
        return np.concatenate(halves(matrix), axis=0)

    first = pack(forward[:, :rows])
    second = pack(forward[:, rows:])
    to_later = stack(inverse[rows:])
    to_first = stack(inverse[:rows])
    to_taps = stack(inverse[rows - np.arange(rows)])
    return first, second, to_later, to_first, to_taps


def passed_along(block, distance):
    devices = range(lax.axis_size(CTX))
    route = [(i - distance, i) for i in devices if i - distance in devices]
    return lax.ppermute(block, CTX, route)


def wide(row_mask, columns):
    return jnp.concatenate([row_mask] * (columns // LANES), axis=1)


def row_ids(rows):
    return lax.broadcasted_iota(jnp.int32, (rows, LANES), 0)


def cuts_of(lengths_ref, rows):
    at = -lax.axis_index(CTX) * rows
    cuts = [at]
    for d in range(lengths_ref.shape[1]):
        at = at + lengths_ref[0, d]
        cuts.append(at)
    return cuts


def begin_at(cuts, at):
    begin = cuts[0]
    for cut in cuts[1:-1]:
        begin = jnp.where(cut <= at, cut, begin)
    return begin


def end_at(cuts, at):
    end = cuts[-1]
    for cut in cuts[-2:0:-1]:
        end = jnp.where(cut > at, cut, end)
    return end


def times(left, right, conjugate_left):
    half = left.shape[0] // 2
    a, b = left[:half], left[half:]
    c, d = right[:half], right[half:]
    if conjugate_left:
        return jnp.concatenate([a * c + b * d, a * d - b * c], axis=0)
    return jnp.concatenate([a * c - b * d, a * d + b * c], axis=0)


def dot(matrix, data):
    return jnp.dot(matrix, jnp.concatenate([data, data], axis=0), preferred_element_type=F32)


def back_dot(matrix, data):
    both = jnp.dot(matrix, data, preferred_element_type=F32)
    half = matrix.shape[0] // 2
    return both[:half] + both[half:]


def on_first_step(fill):
    pl.when(pl.program_id(0) == 0)(fill)


def mix_kernel(lengths_ref, v_ref, before_ref, gs_ref, taps_ref, mixed_ref, short_ref, ext, reach_s):
    rows, columns = v_ref.shape

    @on_first_step
    def _():
        at = row_ids(rows)
        reach_s[...] = at - begin_at(cuts_of(lengths_ref, rows), at)

    ext[0:RIM, :] = before_ref[...].astype(F32)
    ext[RIM:, :] = v_ref[...].astype(F32)
    reach = wide(reach_s[...], columns)
    total = taps_ref[0:1, :] * ext[RIM:, :]
    for j in range(1, taps_ref.shape[0]):
        window = ext[RIM - j : RIM - j + rows, :]
        total = total + taps_ref[j : j + 1, :] * jnp.where(reach >= j, window, 0.0)
    short_ref[...] = total
    mixed_ref[...] = (gs_ref[...].astype(F32) * total).astype(BF)


def own_kernel(lengths_ref, mixed_ref, adj_ref, ltaps_ref, first_ref, second_ref, later_ref,
               front_ref, totaps_ref, long_ref, back_ref, grads_ref, taps_spec, spec_acc, cuts_s):
    rows, columns = mixed_ref.shape
    cuts = cuts_of(lengths_ref, rows)
    low, high = -1, -1
    for d, cut in enumerate(cuts):
        cuts_s[d] = cut
        if d < len(cuts) - 1:
            low = low + (cut <= 0).astype(jnp.int32)
            high = high + (cut <= rows - 1).astype(jnp.int32)
    taps_spec[...] = dot(first_ref[...], ltaps_ref[...].astype(BF))
    long_ref[...] = jnp.zeros_like(long_ref)
    back_ref[...] = jnp.zeros_like(back_ref)
    spec_acc[...] = jnp.zeros_like(spec_acc)
    at = row_ids(rows)

    def document(d, carry):
        inside = jnp.where((at >= cuts_s[d]) & (at < cuts_s[d + 1]), 1.0, 0.0)
        own = wide(inside, columns)
        own_bf = wide(inside.astype(BF), columns)
        x_spec = dot(second_ref[...], mixed_ref[...] * own_bf)
        product = times(taps_spec[...], x_spec, False).astype(BF)
        long_ref[...] += own * back_dot(later_ref[...], product)
        a_spec = dot(first_ref[...], adj_ref[...] * own_bf)
        spec_acc[...] += times(a_spec, x_spec, True)
        product = times(taps_spec[...], a_spec, True).astype(BF)
        back_ref[...] += own * back_dot(front_ref[...], product)
        return carry

    lax.fori_loop(low, high + 1, document, 0)
    grads_ref[...] = back_dot(totaps_ref[...], spec_acc[...].astype(BF))


def grad_kernel(lengths_ref, v_ref, before_ref, gs_ref, adj_ref, short_ref, back_ref, own_grads_ref,
                prev_ref, next_ref, staps_ref, ltaps_ref, first_ref, second_ref, front_ref, totaps_ref,
                ggs_ref, adjs_ref, head_ref, grads_ref, ext, reach_s, masks_s):
    rows, columns = v_ref.shape

    @on_first_step
    def _():
        at = row_ids(rows)
        cuts = cuts_of(lengths_ref, rows)
        reach_s[...] = at - begin_at(cuts, at)
        ones = lambda mask: jnp.where(mask, 1.0, 0.0).astype(BF)
        masks_s[0 * rows : 1 * rows, :] = ones(at < end_at(cuts, 0))
        masks_s[1 * rows : 2 * rows, :] = ones(at - rows >= begin_at(cuts, 0))
        masks_s[2 * rows : 3 * rows, :] = ones(at >= begin_at(cuts, rows - 1))
        masks_s[3 * rows : 4 * rows, :] = ones(at + rows < end_at(cuts, rows - 1))

    mask = lambda k: wide(masks_s[k * rows : (k + 1) * rows, :], columns)
    taps_spec = dot(first_ref[...], ltaps_ref[...].astype(BF))
    next_spec = dot(second_ref[...], next_ref[...] * mask(3))
    product = times(taps_spec, next_spec, True).astype(BF)
    back = back_ref[...] + mask(2).astype(F32) * back_dot(front_ref[...], product)
    prev_spec = dot(first_ref[...], prev_ref[...] * mask(1))
    own_spec = dot(first_ref[...], adj_ref[...] * mask(0))
    product = times(own_spec, prev_spec, True).astype(BF)
    long_terms = own_grads_ref[...] + back_dot(totaps_ref[...], product)

    ggs_ref[...] = (back * short_ref[...]).astype(BF)
    adj_short = (back * gs_ref[...].astype(F32)).astype(BF)
    adjs_ref[...] = adj_short
    adj_short = adj_short.astype(F32)
    head_ref[...] = adj_short[0:RIM].astype(BF)
    ext[0:RIM, :] = before_ref[...].astype(F32)
    ext[RIM:, :] = v_ref[...].astype(F32)
    reach = wide(reach_s[...], columns)
    terms = [jnp.sum(adj_short * ext[RIM:, :], axis=0, keepdims=True)]
    for j in range(1, staps_ref.shape[0]):
        window = ext[RIM - j : RIM - j + rows, :]
        terms.append(jnp.sum(jnp.where(reach >= j, adj_short * window, 0.0), axis=0, keepdims=True))
    terms.append(jnp.zeros((RIM - len(terms), columns), F32))
    terms = jnp.concatenate([long_terms] + terms, axis=0).astype(BF)
    for k in range(columns // LANES):
        grads_ref[k] = terms[:, k * LANES : (k + 1) * LANES]


def long_kernel(lengths_ref, gl_ref, up_ref, long_ref, prev_ref, ltaps_ref, first_ref, later_ref,
                out_ref, ggl_ref, masks_s):
    rows, columns = gl_ref.shape

    @on_first_step
    def _():
        at = row_ids(rows)
        cuts = cuts_of(lengths_ref, rows)
        ones = lambda mask: jnp.where(mask, 1.0, 0.0).astype(BF)
        masks_s[0 * rows : 1 * rows, :] = ones(at < end_at(cuts, 0))
        masks_s[1 * rows : 2 * rows, :] = ones(at - rows >= begin_at(cuts, 0))

    mask = lambda k: wide(masks_s[k * rows : (k + 1) * rows, :], columns)
    taps_spec = dot(first_ref[...], ltaps_ref[...].astype(BF))
    prev_spec = dot(first_ref[...], prev_ref[...] * mask(1))
    product = times(taps_spec, prev_spec, False).astype(BF)
    long_mix = long_ref[...] + mask(0).astype(F32) * back_dot(later_ref[...], product)
    out_ref[...] = (gl_ref[...].astype(F32) * long_mix).astype(BF)
    ggl_ref[...] = (up_ref[...].astype(F32) * long_mix).astype(BF)


def values_kernel(lengths_ref, adjs_ref, after_ref, taps_ref, gv_ref, move):
    rows, columns = adjs_ref.shape
    count = taps_ref.shape[0]

    @on_first_step
    def _():
        at = lax.broadcasted_iota(jnp.int32, (rows, 2 * LANES), 0)
        source = lax.broadcasted_iota(jnp.int32, (rows, 2 * LANES), 1)
        left = end_at(cuts_of(lengths_ref, rows), at) - at
        for j in range(count):
            move[j * rows : (j + 1) * rows, :] = jnp.where(
                (source == at + j) & (left > j), 1.0, 0.0).astype(BF)

    rim = jnp.concatenate([after_ref[...].astype(F32), jnp.zeros((LANES - RIM, columns), F32)], axis=0)
    data = jnp.concatenate([adjs_ref[...], rim.astype(BF)], axis=0)
    moved = jnp.dot(move[...], data, preferred_element_type=F32)
    total = taps_ref[0:1, :] * moved[:rows]
    for j in range(1, count):
        total = total + taps_ref[j : j + 1, :] * moved[j * rows : (j + 1) * rows]
    gv_ref[...] = total.astype(BF)


def spread_kernel(mine_ref, other_ref, short_ref, long_ref):
    rows = long_ref.shape[0]

    def write(blocks):
        for k in range(blocks.shape[0]):
            shares = blocks[k].astype(F32)
            at = slice(k * LANES, (k + 1) * LANES)
            long_ref[:, at] = shares[:rows]
            short_ref[:, at] = shares[rows : rows + short_ref.shape[0]]

    own_turn = pl.program_id(0) == lax.axis_index("core")
    pl.when(own_turn)(lambda: write(mine_ref))
    pl.when(jnp.logical_not(own_turn))(lambda: write(other_ref))


def kernels(rows, channels, count):
    shaped = lambda r, t: jax.ShapeDtypeStruct((r, channels), t)
    first, second, later, front, totaps = [jnp.asarray(m) for m in spectra(rows)]
    parts = channels // LANES

    def call(kernel, parts_per_step, ins, outs, scratch, cost, arrays, mib):
        columns = parts_per_step * LANES

        def spec(shape):
            if shape is None:
                return pl.BlockSpec(memory_space=pltpu.SMEM)
            if isinstance(shape, int):
                return pl.BlockSpec((shape, columns), lambda i: (0, i))
            if len(shape) == 2 and shape[1] == LANES:
                return pl.BlockSpec((parts // 2,) + shape, lambda i: (0, 0, 0))
            if len(shape) == 3:
                return pl.BlockSpec((parts_per_step,) + shape[1:], lambda i: (i, 0, 0))
            return pl.BlockSpec(shape, lambda i: (0, 0))

        return pl.pallas_call(
            kernel,
            grid=(parts // parts_per_step,),
            in_specs=[spec(i) for i in ins],
            out_specs=[spec(o.shape[0] if len(o.shape) == 2 else o.shape) for o in outs],
            out_shape=outs,
            scratch_shapes=[pltpu.VMEM((r, c if c else columns), t) if r else t for r, c, t in scratch],
            compiler_params=pltpu.CompilerParams(vmem_limit_bytes=mib << 20),
            cost_estimate=pl.CostEstimate(
                flops=0, bytes_accessed=int(cost * 3.5e6), transcendentals=0),
        )(*arrays)

    small = min(8, parts // 2)
    large = min(16, parts // 2)
    ext = (rows + RIM, 0, F32)
    spectrum = (2 * rows, 0, F32)
    tables = lambda *chosen: [t.shape for t in chosen]
    grads_shape = jax.ShapeDtypeStruct((parts, rows + RIM, LANES), BF)

    def mix(*arrays):
        return call(mix_kernel, small, [None, rows, RIM, rows, count],
                    [shaped(rows, BF), shaped(rows, F32)], [ext, (rows, LANES, jnp.int32)], 6, arrays, 56)

    def own(*arrays):
        used = (first, second, later, front, totaps)
        return call(own_kernel, large, [None, rows, rows, rows] + tables(*used),
                    [shaped(rows, F32)] * 3,
                    [spectrum, spectrum, (0, 0, pltpu.SMEM((16,), jnp.int32))], 15, arrays + used, 40)

    def grad(*arrays):
        used = (first, second, front, totaps)
        return call(grad_kernel, small, [None, rows, RIM] + [rows] * 7 + [count, rows] + tables(*used),
                    [shaped(rows, BF), shaped(rows, BF), shaped(RIM, BF), grads_shape],
                    [ext, (rows, LANES, jnp.int32), (4 * rows, LANES, BF)], 12, arrays + used, 30)

    def long(*arrays):
        used = (first, later)
        return call(long_kernel, large, [None] + [rows] * 5 + tables(*used),
                    [shaped(rows, BF)] * 2, [(2 * rows, LANES, BF)], 6, arrays + used, 32)

    def values_grad(*arrays):
        return call(values_kernel, large, [None, rows, RIM, count], [shaped(rows, BF)],
                    [(count * rows, 2 * LANES, BF)], 4, arrays, 24)[0]

    def spread(mine, other):
        return call(spread_kernel, parts // 2, [mine.shape[1:], other.shape[1:]],
                    [shaped(count, F32), shaped(rows, F32)], [], 3, (mine, other), 24)

    return mix, own, grad, long, values_grad, spread


def traded(block, axes):
    return lax.all_to_all(block, axes, 0, 0, tiled=True)


def copies(block, axes):
    return traded(jnp.broadcast_to(block[None], (lax.axis_size(axes),) + block.shape), axes)


def added(blocks):
    return jnp.sum(blocks.astype(F32), axis=0)


def swapped(block):
    return lax.ppermute(block, "core", [(0, 1), (1, 0)])


def on_device(lengths, values, gate_short, gate_long, short_taps, long_taps, cotangent):
    v, gs, gl, up = values[0], gate_short[0], gate_long[0], cotangent[0]
    rows, channels = v.shape
    mix, own, grad, long, values_grad, spread = kernels(rows, channels, short_taps.shape[0])
    factor = 1.0 / math.sqrt(lax.axis_size(("y", "core", "z", "x")) * rows)

    before = passed_along(v[rows - RIM :], 1)
    adj = (up.astype(F32) * gl.astype(F32)).astype(BF)
    following = passed_along(adj, -1)
    mixed, short = mix(lengths, v, before, gs, short_taps)
    prev = passed_along(mixed, 1)
    own_long, own_back, own_grads = own(lengths, mixed, adj, long_taps)
    ggs, adjs, head, grads = grad(lengths, v, before, gs, adj, short, own_back, own_grads,
                                  prev, following, short_taps, long_taps)
    after = passed_along(head, -1)

    core = lax.axis_index("core")
    planes = ("y", "x")
    split = grads.reshape((2, grads.shape[0] // 2) + grads.shape[1:])
    pick = lambda i: lax.dynamic_index_in_dim(split, i, 0, keepdims=False)
    half = (pick(core).astype(F32) + swapped(pick(1 - core)).astype(F32)).astype(BF)
    half, own_long, adjs = lax.optimization_barrier((half, own_long, adjs))
    share = half.reshape((lax.axis_size(planes), -1) + half.shape[1:])
    share = added(traded(share, planes)).astype(BF)
    out, ggl = long(lengths, gl, up, own_long, prev, long_taps)
    share, out, ggl, adjs = lax.optimization_barrier((share, out, ggl, adjs))
    share = (added(copies(share, "z")) * factor).astype(BF)
    gv = values_grad(lengths, adjs, after, short_taps)
    share, gv = lax.optimization_barrier((share, gv))
    mine = copies(share, planes).reshape(half.shape)
    grad_short, grad_long = spread(mine, swapped(mine))
    return out[None], ggs[None], gv[None], ggl[None], grad_short, grad_long


def solution(mesh):
    dp, ctx = mesh.shape["dp"], mesh.shape["ctx"]
    cut = jax.sharding.Mesh(mesh.devices.reshape(dp // 2, 2, ctx // 4, 4), ("y", "core", "z", "x"))
    rowed = P(("y", "core"), CTX, None)
    return jax.shard_map(
        on_device,
        mesh=cut,
        in_specs=(P(("y", "core"), None), rowed, rowed, rowed, P(), P(), rowed),
        out_specs=(rowed, rowed, rowed, rowed, P(), P()),
        check_vma=False,
    )
```

```python
import math

import jax
import jax.numpy as jnp
import numpy as np
from jax import lax
from jax.experimental import pallas as pl
from jax.experimental.pallas import tpu as pltpu
from jax.sharding import PartitionSpec as P

BF = jnp.bfloat16
F32 = jnp.float32
LANES = 128
RIM = 8
CTX = ("z", "x")


def halves(matrix):
    high = matrix.astype(np.float32).astype(BF)
    low = (matrix - high.astype(np.float64)).astype(np.float32).astype(BF)
    return high, low


def spectra(rows):
    points = 2 * rows
    theta = np.pi * (2 * np.arange(rows) + 1) / points
    angles = theta[:, None] * np.arange(points)[None, :]
    forward = np.concatenate([np.cos(angles), -np.sin(angles)], axis=0)
    inverse = forward.T / rows

    def pack(matrix):
        return np.concatenate(halves(matrix), axis=1)

    def stack(matrix):
        return np.concatenate(halves(matrix), axis=0)

    first = pack(forward[:, :rows])
    second = pack(forward[:, rows:])
    to_later = stack(inverse[rows:])
    to_first = stack(inverse[:rows])
    to_taps = stack(inverse[rows - np.arange(rows)])
    return first, second, to_later, to_first, to_taps


def passed_along(block, distance):
    devices = range(lax.axis_size(CTX))
    route = [(i - distance, i) for i in devices if i - distance in devices]
    return lax.ppermute(block, CTX, route)


def wide(row_mask, columns):
    return jnp.concatenate([row_mask] * (columns // LANES), axis=1)


def row_ids(rows):
    return lax.broadcasted_iota(jnp.int32, (rows, LANES), 0)


def cuts_of(lengths_ref, rows):
    at = -lax.axis_index(CTX) * rows
    cuts = [at]
    for d in range(lengths_ref.shape[1]):
        at = at + lengths_ref[0, d]
        cuts.append(at)
    return cuts


def begin_at(cuts, at):
    begin = cuts[0]
    for cut in cuts[1:-1]:
        begin = jnp.where(cut <= at, cut, begin)
    return begin


def end_at(cuts, at):
    end = cuts[-1]
    for cut in cuts[-2:0:-1]:
        end = jnp.where(cut > at, cut, end)
    return end


def times(left, right, conjugate_left):
    half = left.shape[0] // 2
    a, b = left[:half], left[half:]
    c, d = right[:half], right[half:]
    if conjugate_left:
        return jnp.concatenate([a * c + b * d, a * d - b * c], axis=0)
    return jnp.concatenate([a * c - b * d, a * d + b * c], axis=0)


def dot(matrix, data):
    return jnp.dot(matrix, jnp.concatenate([data, data], axis=0), preferred_element_type=F32)


def back_dot(matrix, data):
    both = jnp.dot(matrix, data, preferred_element_type=F32)
    half = matrix.shape[0] // 2
    return both[:half] + both[half:]


def on_first_step(fill):
    pl.when(pl.program_id(0) == 0)(fill)


def mix_kernel(half_ref, lengths_ref, v_ref, before_ref, gs_ref, taps_ref, mixed_ref, short_ref, ext, reach_s):
    rows, columns = v_ref.shape

    @on_first_step
    def _():
        at = row_ids(rows)
        reach_s[...] = at - begin_at(cuts_of(lengths_ref, rows), at)

    ext[0:RIM, :] = before_ref[...].astype(F32)
    ext[RIM:, :] = v_ref[...].astype(F32)
    reach = wide(reach_s[...], columns)
    total = taps_ref[0:1, :] * ext[RIM:, :]
    for j in range(1, taps_ref.shape[0]):
        window = ext[RIM - j : RIM - j + rows, :]
        total = total + taps_ref[j : j + 1, :] * jnp.where(reach >= j, window, 0.0)
    short_ref[...] = total
    mixed_ref[...] = (gs_ref[...].astype(F32) * total).astype(BF)


def own_kernel(half_ref, lengths_ref, mixed_ref, adj_ref, ltaps_ref, first_ref, second_ref, later_ref,
               front_ref, totaps_ref, long_ref, back_ref, grads_ref, taps_spec, spec_acc, cuts_s):
    rows, columns = mixed_ref.shape
    cuts = cuts_of(lengths_ref, rows)
    low, high = -1, -1
    for d, cut in enumerate(cuts):
        cuts_s[d] = cut
        if d < len(cuts) - 1:
            low = low + (cut <= 0).astype(jnp.int32)
            high = high + (cut <= rows - 1).astype(jnp.int32)
    taps_spec[...] = dot(first_ref[...], ltaps_ref[...].astype(BF))
    long_ref[...] = jnp.zeros_like(long_ref)
    back_ref[...] = jnp.zeros_like(back_ref)
    spec_acc[...] = jnp.zeros_like(spec_acc)
    at = row_ids(rows)

    def document(d, carry):
        inside = jnp.where((at >= cuts_s[d]) & (at < cuts_s[d + 1]), 1.0, 0.0)
        own = wide(inside, columns)
        own_bf = wide(inside.astype(BF), columns)
        x_spec = dot(second_ref[...], mixed_ref[...] * own_bf)
        product = times(taps_spec[...], x_spec, False).astype(BF)
        long_ref[...] += own * back_dot(later_ref[...], product)
        a_spec = dot(first_ref[...], adj_ref[...] * own_bf)
        spec_acc[...] += times(a_spec, x_spec, True)
        product = times(taps_spec[...], a_spec, True).astype(BF)
        back_ref[...] += own * back_dot(front_ref[...], product)
        return carry

    lax.fori_loop(low, high + 1, document, 0)
    grads_ref[...] = back_dot(totaps_ref[...], spec_acc[...].astype(BF))


def grad_kernel(half_ref, lengths_ref, v_ref, before_ref, gs_ref, adj_ref, short_ref, back_ref, own_grads_ref,
                prev_ref, next_ref, staps_ref, ltaps_ref, first_ref, second_ref, front_ref, totaps_ref, *rest):
    ggs_ref, adjs_ref, head_ref, grads_ref, ext, reach_s, masks_s = rest[-7:]
    rows, columns = v_ref.shape

    @on_first_step
    def _():
        at = row_ids(rows)
        cuts = cuts_of(lengths_ref, rows)
        reach_s[...] = at - begin_at(cuts, at)
        ones = lambda mask: jnp.where(mask, 1.0, 0.0).astype(BF)
        masks_s[0 * rows : 1 * rows, :] = ones(at < end_at(cuts, 0))
        masks_s[1 * rows : 2 * rows, :] = ones(at - rows >= begin_at(cuts, 0))
        masks_s[2 * rows : 3 * rows, :] = ones(at >= begin_at(cuts, rows - 1))
        masks_s[3 * rows : 4 * rows, :] = ones(at + rows < end_at(cuts, rows - 1))

    mask = lambda k: wide(masks_s[k * rows : (k + 1) * rows, :], columns)
    taps_spec = dot(first_ref[...], ltaps_ref[...].astype(BF))
    next_spec = dot(second_ref[...], next_ref[...] * mask(3))
    product = times(taps_spec, next_spec, True).astype(BF)
    back = back_ref[...] + mask(2).astype(F32) * back_dot(front_ref[...], product)
    prev_spec = dot(first_ref[...], prev_ref[...] * mask(1))
    own_spec = dot(first_ref[...], adj_ref[...] * mask(0))
    product = times(own_spec, prev_spec, True).astype(BF)
    long_terms = own_grads_ref[...] + back_dot(totaps_ref[...], product)

    ggs_ref[...] = (back * short_ref[...]).astype(BF)
    adj_short = (back * gs_ref[...].astype(F32)).astype(BF)
    adjs_ref[...] = adj_short
    adj_short = adj_short.astype(F32)
    head_ref[...] = adj_short[0:RIM].astype(BF)
    ext[0:RIM, :] = before_ref[...].astype(F32)
    ext[RIM:, :] = v_ref[...].astype(F32)
    reach = wide(reach_s[...], columns)
    terms = [jnp.sum(adj_short * ext[RIM:, :], axis=0, keepdims=True)]
    for j in range(1, staps_ref.shape[0]):
        window = ext[RIM - j : RIM - j + rows, :]
        terms.append(jnp.sum(jnp.where(reach >= j, adj_short * window, 0.0), axis=0, keepdims=True))
    terms.append(jnp.zeros((RIM - len(terms), columns), F32))
    terms = jnp.concatenate([long_terms] + terms, axis=0).astype(BF)
    for k in range(columns // LANES):
        grads_ref[k] = terms[:, k * LANES : (k + 1) * LANES]


def long_kernel(half_ref, lengths_ref, gl_ref, up_ref, long_ref, prev_ref, ltaps_ref, first_ref, later_ref, *rest):
    out_ref, ggl_ref, masks_s = rest[-3:]
    rows, columns = gl_ref.shape

    @on_first_step
    def _():
        at = row_ids(rows)
        cuts = cuts_of(lengths_ref, rows)
        ones = lambda mask: jnp.where(mask, 1.0, 0.0).astype(BF)
        masks_s[0 * rows : 1 * rows, :] = ones(at < end_at(cuts, 0))
        masks_s[1 * rows : 2 * rows, :] = ones(at - rows >= begin_at(cuts, 0))

    mask = lambda k: wide(masks_s[k * rows : (k + 1) * rows, :], columns)
    taps_spec = dot(first_ref[...], ltaps_ref[...].astype(BF))
    prev_spec = dot(first_ref[...], prev_ref[...] * mask(1))
    product = times(taps_spec, prev_spec, False).astype(BF)
    long_mix = long_ref[...] + mask(0).astype(F32) * back_dot(later_ref[...], product)
    out_ref[...] = (gl_ref[...].astype(F32) * long_mix).astype(BF)
    ggl_ref[...] = (up_ref[...].astype(F32) * long_mix).astype(BF)


def values_kernel(lengths_ref, adjs_ref, after_ref, taps_ref, gv_ref, move):
    rows, columns = adjs_ref.shape
    count = taps_ref.shape[0]

    @on_first_step
    def _():
        at = lax.broadcasted_iota(jnp.int32, (rows, 2 * LANES), 0)
        source = lax.broadcasted_iota(jnp.int32, (rows, 2 * LANES), 1)
        left = end_at(cuts_of(lengths_ref, rows), at) - at
        for j in range(count):
            move[j * rows : (j + 1) * rows, :] = jnp.where(
                (source == at + j) & (left > j), 1.0, 0.0).astype(BF)

    rim = jnp.concatenate([after_ref[...].astype(F32), jnp.zeros((LANES - RIM, columns), F32)], axis=0)
    data = jnp.concatenate([adjs_ref[...], rim.astype(BF)], axis=0)
    moved = jnp.dot(move[...], data, preferred_element_type=F32)
    total = taps_ref[0:1, :] * moved[:rows]
    for j in range(1, count):
        total = total + taps_ref[j : j + 1, :] * moved[j * rows : (j + 1) * rows]
    gv_ref[...] = total.astype(BF)


def spread_kernel(mine_ref, other_ref, short_ref, long_ref):
    rows = long_ref.shape[0]

    def write(blocks):
        for k in range(blocks.shape[0]):
            shares = blocks[k].astype(F32)
            at = slice(k * LANES, (k + 1) * LANES)
            long_ref[:, at] = shares[:rows]
            short_ref[:, at] = shares[rows : rows + short_ref.shape[0]]

    own_turn = pl.program_id(0) == lax.axis_index("core")
    pl.when(own_turn)(lambda: write(mine_ref))
    pl.when(jnp.logical_not(own_turn))(lambda: write(other_ref))


class Kernels:

    def __init__(self, rows, channels, count):
        self.rows, self.channels, self.count = rows, channels, count
        self.parts = channels // LANES
        self.tables = [jnp.asarray(m) for m in spectra(rows)]

    def call(self, kernel, step_parts, half, ins, outs, scratch, cost, mib, filled=()):
        columns = step_parts * LANES
        steps = self.parts // step_parts
        if half is not None:
            steps //= 2

        def spec(kind, shape):
            if kind == "scalars":
                return pl.BlockSpec(memory_space=pltpu.SMEM)
            if kind == "table":
                return pl.BlockSpec(shape, lambda i, *h: (0,) * len(shape))
            if kind == "shares":
                return pl.BlockSpec((step_parts,) + shape[1:], lambda i, *h: (i, 0, 0))
            if kind == "whole" and half is not None:
                return pl.BlockSpec((shape[0], columns), lambda i, h: (0, h[0] * steps + i))
            return pl.BlockSpec((shape[0], columns), lambda i, *h: (0, i))

        prefetch = 0 if half is None else 1
        arrays = ([] if half is None else [half]) + [a for _, a in ins] + list(filled)
        in_specs = [spec(k, a.shape) for k, a in ins] + [pl.BlockSpec(memory_space=pl.ANY)] * len(filled)
        return pl.pallas_call(
            kernel,
            grid_spec=pltpu.PrefetchScalarGridSpec(
                num_scalar_prefetch=prefetch,
                grid=(steps,),
                in_specs=in_specs,
                out_specs=[spec(k, o.shape) for k, o in outs],
                scratch_shapes=[pltpu.VMEM((r, c if c else columns), t) if r else t for r, c, t in scratch],
            ),
            out_shape=[o for _, o in outs],
            input_output_aliases={prefetch + len(ins) + k: k for k in range(len(filled))},
            compiler_params=pltpu.CompilerParams(vmem_limit_bytes=mib << 20),
            cost_estimate=pl.CostEstimate(
                flops=0, bytes_accessed=int(cost * 3.5e6), transcendentals=0),
        )(*arrays)

    def shaped(self, rows, kind):
        width = self.channels // 2 if kind == "half" else self.channels
        return lambda t: (kind, jax.ShapeDtypeStruct((rows, width), t))

    def small(self):
        return min(8, self.parts // 4)

    def mix(self, half, lengths, v, before, gs, staps):
        out = self.shaped(self.rows, "half")
        return self.call(
            mix_kernel, self.small(), half,
            [("scalars", lengths), ("whole", v), ("whole", before), ("whole", gs), ("whole", staps)],
            [out(BF), out(F32)],
            [(self.rows + RIM, 0, F32), (self.rows, LANES, jnp.int32)], 3, 20)

    def own(self, half, lengths, mixed, adj, ltaps):
        out = self.shaped(self.rows, "half")
        spectrum = (2 * self.rows, 0, F32)
        return self.call(
            own_kernel, self.small(), half,
            [("scalars", lengths), ("half", mixed), ("whole", adj), ("whole", ltaps)]
            + [("table", t) for t in self.tables],
            [out(F32)] * 3,
            [spectrum, spectrum, (0, 0, pltpu.SMEM((16,), jnp.int32))], 1.5, 28)

    def grad(self, half, lengths, v, before, gs, adj, short, back, own_grads, prev, following,
             staps, ltaps, filled):
        first, second, _, front, totaps = self.tables
        rows = self.rows
        out = self.shaped(rows, "whole")
        grads = jax.ShapeDtypeStruct((self.parts // 2, rows + RIM, LANES), BF)
        return self.call(
            grad_kernel, self.small(), half,
            [("scalars", lengths), ("whole", v), ("whole", before), ("whole", gs), ("whole", adj),
             ("half", short), ("half", back), ("half", own_grads), ("half", prev),
             ("whole", following), ("whole", staps), ("whole", ltaps)]
            + [("table", t) for t in (first, second, front, totaps)],
            [out(BF), out(BF), self.shaped(RIM, "whole")(BF), ("shares", grads)],
            [(rows + RIM, 0, F32), (rows, LANES, jnp.int32), (4 * rows, LANES, BF)], 1.5, 28, filled)

    def long(self, half, lengths, gl, up, own_long, prev, ltaps, filled):
        out = self.shaped(self.rows, "whole")
        return self.call(
            long_kernel, self.small(), half,
            [("scalars", lengths), ("whole", gl), ("whole", up), ("half", own_long), ("half", prev),
             ("whole", ltaps), ("table", self.tables[0]), ("table", self.tables[2])],
            [out(BF)] * 2, [(2 * self.rows, LANES, BF)], 3, 24, filled)

    def values_grad(self, lengths, adjs, after, staps):
        return self.call(
            values_kernel, 2 * self.small(), None,
            [("scalars", lengths), ("whole", adjs), ("whole", after), ("whole", staps)],
            [self.shaped(self.rows, "whole")(BF)],
            [(self.count * self.rows, 2 * LANES, BF)], 4, 24)[0]

    def spread(self, mine, other):
        return self.call(
            spread_kernel, self.parts // 2, None, [("table", mine), ("table", other)],
            [self.shaped(self.count, "whole")(F32), self.shaped(self.rows, "whole")(F32)], [], 3, 24)


def traded(block, axes):
    return lax.all_to_all(block, axes, 0, 0, tiled=True)


def copies(block, axes):
    return traded(jnp.broadcast_to(block[None], (lax.axis_size(axes),) + block.shape), axes)


def added(blocks):
    return jnp.sum(blocks.astype(F32), axis=0)


def swapped(block):
    return lax.ppermute(block, "core", [(0, 1), (1, 0)])


def on_device(lengths, values, gate_short, gate_long, short_taps, long_taps, cotangent):
    v, gs, gl, up = values[0], gate_short[0], gate_long[0], cotangent[0]
    rows, channels = v.shape
    k = Kernels(rows, channels, short_taps.shape[0])
    factor = 1.0 / math.sqrt(lax.axis_size(("y", "core", "z", "x")) * rows)
    together = lax.optimization_barrier

    core = lax.axis_index("core").astype(jnp.int32)
    kept = core[None]
    given = 1 - kept

    before = passed_along(v[rows - RIM :], 1)
    adj = (up.astype(F32) * gl.astype(F32)).astype(BF)
    following = passed_along(adj, -1)
    mixed_a, short_a = k.mix(given, lengths, v, before, gs, short_taps)
    prev_a = passed_along(mixed_a, 1)
    mixed_b, short_b = k.mix(kept, lengths, v, before, gs, short_taps)
    long_a, back_a, terms_a = k.own(given, lengths, mixed_a, adj, long_taps)
    mixed_b, back_a = together((mixed_b, back_a))
    prev_b = passed_along(mixed_b, 1)
    long_b, back_b, terms_b = k.own(kept, lengths, mixed_b, adj, long_taps)
    prev_a, back_b = together((prev_a, back_b))
    ggs, adjs, head, grads_a = k.grad(given, lengths, v, before, gs, adj, short_a, back_a, terms_a,
                                      prev_a, following, short_taps, long_taps, ())
    grads_a, prev_b = together((grads_a, prev_b))
    got = swapped(grads_a)
    ggs, adjs, head, grads_b = k.grad(kept, lengths, v, before, gs, adj, short_b, back_b, terms_b,
                                      prev_b, following, short_taps, long_taps, (ggs, adjs, head))

    planes = ("y", "x")
    half = (grads_b.astype(F32) + got.astype(F32)).astype(BF)
    half, long_a, adjs, head = together((half, long_a, adjs, head))
    share = half.reshape((lax.axis_size(planes), -1) + half.shape[1:])
    share = added(traded(share, planes)).astype(BF)
    out_ggl = k.long(given, lengths, gl, up, long_a, prev_a, long_taps, ())
    out, ggl = k.long(kept, lengths, gl, up, long_b, prev_b, long_taps, tuple(out_ggl))
    share, out, ggl, adjs, head = together((share, out, ggl, adjs, head))
    after = passed_along(head, -1)
    share = (added(copies(share, "z")) * factor).astype(BF)
    share, after, adjs = together((share, after, adjs))
    mine = copies(share, planes).reshape(half.shape)
    gv = k.values_grad(lengths, adjs, after, short_taps)
    mine, gv = together((mine, gv))
    grad_short, grad_long = k.spread(mine, swapped(mine))
    return out[None], ggs[None], gv[None], ggl[None], grad_short, grad_long


def solution(mesh):
    dp, ctx = mesh.shape["dp"], mesh.shape["ctx"]
    cut = jax.sharding.Mesh(mesh.devices.reshape(dp // 2, 2, ctx // 4, 4), ("y", "core", "z", "x"))
    rowed = P(("y", "core"), CTX, None)
    return jax.shard_map(
        on_device,
        mesh=cut,
        in_specs=(P(("y", "core"), None), rowed, rowed, rowed, P(), P(), rowed),
        out_specs=(rowed, rowed, rowed, rowed, P(), P()),
        check_vma=False,
    )
```

```python
import math

import jax
import jax.numpy as jnp
import numpy as np
from jax import lax
from jax.experimental import pallas as pl
from jax.experimental.pallas import tpu as pltpu
from jax.sharding import PartitionSpec as P

BF = jnp.bfloat16
F32 = jnp.float32
LANES = 128
RIM = 8
CTX = ("z", "x")


def halves(matrix):
    high = matrix.astype(np.float32).astype(BF)
    low = (matrix - high.astype(np.float64)).astype(np.float32).astype(BF)
    return high, low


def spectra(rows):
    points = 2 * rows
    theta = np.pi * (2 * np.arange(rows) + 1) / points
    angles = theta[:, None] * np.arange(points)[None, :]
    forward = np.concatenate([np.cos(angles), -np.sin(angles)], axis=0)
    inverse = forward.T / rows

    def pack(matrix):
        return np.concatenate(halves(matrix), axis=1)

    def stack(matrix):
        return np.concatenate(halves(matrix), axis=0)

    first = pack(forward[:, :rows])
    second = pack(forward[:, rows:])
    to_later = stack(inverse[rows:])
    to_first = stack(inverse[:rows])
    to_taps = stack(inverse[rows - np.arange(rows)])
    return first, second, to_later, to_first, to_taps


def passed_along(block, distance):
    devices = range(lax.axis_size(CTX))
    route = [(i - distance, i) for i in devices if i - distance in devices]
    return lax.ppermute(block, CTX, route)


def wide(row_mask, columns):
    return jnp.concatenate([row_mask] * (columns // LANES), axis=1)


def row_ids(rows):
    return lax.broadcasted_iota(jnp.int32, (rows, LANES), 0)


def cuts_of(lengths_ref, rows):
    at = -lax.axis_index(CTX) * rows
    cuts = [at]
    for d in range(lengths_ref.shape[1]):
        at = at + lengths_ref[0, d]
        cuts.append(at)
    return cuts


def begin_at(cuts, at):
    begin = cuts[0]
    for cut in cuts[1:-1]:
        begin = jnp.where(cut <= at, cut, begin)
    return begin


def end_at(cuts, at):
    end = cuts[-1]
    for cut in cuts[-2:0:-1]:
        end = jnp.where(cut > at, cut, end)
    return end


def times(left, right, conjugate_left):
    half = left.shape[0] // 2
    a, b = left[:half], left[half:]
    c, d = right[:half], right[half:]
    if conjugate_left:
        return jnp.concatenate([a * c + b * d, a * d - b * c], axis=0)
    return jnp.concatenate([a * c - b * d, a * d + b * c], axis=0)


def dot(matrix, data):
    return jnp.dot(matrix, jnp.concatenate([data, data], axis=0), preferred_element_type=F32)


def back_dot(matrix, data):
    both = jnp.dot(matrix, data, preferred_element_type=F32)
    half = matrix.shape[0] // 2
    return both[:half] + both[half:]


def on_first_step(fill):
    pl.when(pl.program_id(0) == 0)(fill)


def mix_kernel(half_ref, lengths_ref, v_ref, before_ref, gs_ref, taps_ref, mixed_ref, short_ref, ext, reach_s):
    rows, columns = v_ref.shape

    @on_first_step
    def _():
        at = row_ids(rows)
        reach_s[...] = at - begin_at(cuts_of(lengths_ref, rows), at)

    ext[0:RIM, :] = before_ref[...].astype(F32)
    ext[RIM:, :] = v_ref[...].astype(F32)
    reach = wide(reach_s[...], columns)
    total = taps_ref[0:1, :] * ext[RIM:, :]
    for j in range(1, taps_ref.shape[0]):
        window = ext[RIM - j : RIM - j + rows, :]
        total = total + taps_ref[j : j + 1, :] * jnp.where(reach >= j, window, 0.0)
    short_ref[...] = total
    mixed_ref[...] = (gs_ref[...].astype(F32) * total).astype(BF)


def own_kernel(half_ref, lengths_ref, mixed_ref, adj_ref, ltaps_ref, first_ref, second_ref, later_ref,
               front_ref, totaps_ref, long_ref, back_ref, grads_ref, taps_spec, spec_acc, cuts_s):
    rows, columns = mixed_ref.shape
    cuts = cuts_of(lengths_ref, rows)
    low, high = -1, -1
    for d, cut in enumerate(cuts):
        cuts_s[d] = cut
        if d < len(cuts) - 1:
            low = low + (cut <= 0).astype(jnp.int32)
            high = high + (cut <= rows - 1).astype(jnp.int32)
    taps_spec[...] = dot(first_ref[...], ltaps_ref[...].astype(BF))
    long_ref[...] = jnp.zeros_like(long_ref)
    back_ref[...] = jnp.zeros_like(back_ref)
    spec_acc[...] = jnp.zeros_like(spec_acc)
    at = row_ids(rows)

    def document(d, carry):
        inside = jnp.where((at >= cuts_s[d]) & (at < cuts_s[d + 1]), 1.0, 0.0)
        own = wide(inside, columns)
        own_bf = wide(inside.astype(BF), columns)
        x_spec = dot(second_ref[...], mixed_ref[...] * own_bf)
        product = times(taps_spec[...], x_spec, False).astype(BF)
        long_ref[...] += own * back_dot(later_ref[...], product)
        a_spec = dot(first_ref[...], adj_ref[...] * own_bf)
        spec_acc[...] += times(a_spec, x_spec, True)
        product = times(taps_spec[...], a_spec, True).astype(BF)
        back_ref[...] += own * back_dot(front_ref[...], product)
        return carry

    lax.fori_loop(low, high + 1, document, 0)
    grads_ref[...] = back_dot(totaps_ref[...], spec_acc[...].astype(BF))


def grad_kernel(half_ref, lengths_ref, v_ref, before_ref, gs_ref, adj_ref, short_ref, back_ref, own_grads_ref,
                prev_ref, next_ref, staps_ref, ltaps_ref, first_ref, second_ref, front_ref, totaps_ref, *rest):
    ggs_ref, adjs_ref, head_ref, grads_ref, ext, reach_s, masks_s = rest[-7:]
    rows, columns = v_ref.shape

    @on_first_step
    def _():
        at = row_ids(rows)
        cuts = cuts_of(lengths_ref, rows)
        reach_s[...] = at - begin_at(cuts, at)
        ones = lambda mask: jnp.where(mask, 1.0, 0.0).astype(BF)
        masks_s[0 * rows : 1 * rows, :] = ones(at < end_at(cuts, 0))
        masks_s[1 * rows : 2 * rows, :] = ones(at - rows >= begin_at(cuts, 0))
        masks_s[2 * rows : 3 * rows, :] = ones(at >= begin_at(cuts, rows - 1))
        masks_s[3 * rows : 4 * rows, :] = ones(at + rows < end_at(cuts, rows - 1))

    mask = lambda k: wide(masks_s[k * rows : (k + 1) * rows, :], columns)
    taps_spec = dot(first_ref[...], ltaps_ref[...].astype(BF))
    next_spec = dot(second_ref[...], next_ref[...] * mask(3))
    product = times(taps_spec, next_spec, True).astype(BF)
    back = back_ref[...] + mask(2).astype(F32) * back_dot(front_ref[...], product)
    prev_spec = dot(first_ref[...], prev_ref[...] * mask(1))
    own_spec = dot(first_ref[...], adj_ref[...] * mask(0))
    product = times(own_spec, prev_spec, True).astype(BF)
    long_terms = own_grads_ref[...] + back_dot(totaps_ref[...], product)

    ggs_ref[...] = (back * short_ref[...]).astype(BF)
    adj_short = (back * gs_ref[...].astype(F32)).astype(BF)
    adjs_ref[...] = adj_short
    adj_short = adj_short.astype(F32)
    head_ref[...] = adj_short[0:RIM].astype(BF)
    ext[0:RIM, :] = before_ref[...].astype(F32)
    ext[RIM:, :] = v_ref[...].astype(F32)
    reach = wide(reach_s[...], columns)
    terms = [jnp.sum(adj_short * ext[RIM:, :], axis=0, keepdims=True)]
    for j in range(1, staps_ref.shape[0]):
        window = ext[RIM - j : RIM - j + rows, :]
        terms.append(jnp.sum(jnp.where(reach >= j, adj_short * window, 0.0), axis=0, keepdims=True))
    terms.append(jnp.zeros((RIM - len(terms), columns), F32))
    terms = jnp.concatenate([long_terms] + terms, axis=0).astype(BF)
    for k in range(columns // LANES):
        grads_ref[k] = terms[:, k * LANES : (k + 1) * LANES]


def long_kernel(half_ref, lengths_ref, gl_ref, up_ref, long_ref, prev_ref, ltaps_ref, first_ref, later_ref, *rest):
    out_ref, ggl_ref, masks_s = rest[-3:]
    rows, columns = gl_ref.shape

    @on_first_step
    def _():
        at = row_ids(rows)
        cuts = cuts_of(lengths_ref, rows)
        ones = lambda mask: jnp.where(mask, 1.0, 0.0).astype(BF)
        masks_s[0 * rows : 1 * rows, :] = ones(at < end_at(cuts, 0))
        masks_s[1 * rows : 2 * rows, :] = ones(at - rows >= begin_at(cuts, 0))

    mask = lambda k: wide(masks_s[k * rows : (k + 1) * rows, :], columns)
    taps_spec = dot(first_ref[...], ltaps_ref[...].astype(BF))
    prev_spec = dot(first_ref[...], prev_ref[...] * mask(1))
    product = times(taps_spec, prev_spec, False).astype(BF)
    long_mix = long_ref[...] + mask(0).astype(F32) * back_dot(later_ref[...], product)
    out_ref[...] = (gl_ref[...].astype(F32) * long_mix).astype(BF)
    ggl_ref[...] = (up_ref[...].astype(F32) * long_mix).astype(BF)


def values_kernel(lengths_ref, adjs_ref, after_ref, taps_ref, gv_ref, move):
    rows, columns = adjs_ref.shape
    count = taps_ref.shape[0]

    @on_first_step
    def _():
        at = lax.broadcasted_iota(jnp.int32, (rows, 2 * LANES), 0)
        source = lax.broadcasted_iota(jnp.int32, (rows, 2 * LANES), 1)
        left = end_at(cuts_of(lengths_ref, rows), at) - at
        for j in range(count):
            move[j * rows : (j + 1) * rows, :] = jnp.where(
                (source == at + j) & (left > j), 1.0, 0.0).astype(BF)

    rim = jnp.concatenate([after_ref[...].astype(F32), jnp.zeros((LANES - RIM, columns), F32)], axis=0)
    data = jnp.concatenate([adjs_ref[...], rim.astype(BF)], axis=0)
    moved = jnp.dot(move[...], data, preferred_element_type=F32)
    total = taps_ref[0:1, :] * moved[:rows]
    for j in range(1, count):
        total = total + taps_ref[j : j + 1, :] * moved[j * rows : (j + 1) * rows]
    gv_ref[...] = total.astype(BF)


def spread_kernel(mine_ref, other_ref, short_ref, long_ref):
    rows = long_ref.shape[0]

    def write(blocks):
        for k in range(blocks.shape[0]):
            shares = blocks[k].astype(F32)
            at = slice(k * LANES, (k + 1) * LANES)
            long_ref[:, at] = shares[:rows]
            short_ref[:, at] = shares[rows : rows + short_ref.shape[0]]

    own_turn = pl.program_id(0) == lax.axis_index("core")
    pl.when(own_turn)(lambda: write(mine_ref))
    pl.when(jnp.logical_not(own_turn))(lambda: write(other_ref))


class Kernels:

    def __init__(self, rows, channels, count):
        self.rows, self.channels, self.count = rows, channels, count
        self.parts = channels // LANES
        self.tables = [jnp.asarray(m) for m in spectra(rows)]

    def call(self, kernel, step_parts, half, ins, outs, scratch, cost, mib, filled=()):
        columns = step_parts * LANES
        steps = self.parts // step_parts
        if half is not None:
            steps //= 2

        def spec(kind, shape):
            if kind == "scalars":
                return pl.BlockSpec(memory_space=pltpu.SMEM)
            if kind == "table":
                return pl.BlockSpec(shape, lambda i, *h: (0,) * len(shape))
            if kind == "shares":
                return pl.BlockSpec((step_parts,) + shape[1:], lambda i, *h: (i, 0, 0))
            if kind == "whole" and half is not None:
                return pl.BlockSpec((shape[0], columns), lambda i, h: (0, h[0] * steps + i))
            return pl.BlockSpec((shape[0], columns), lambda i, *h: (0, i))

        prefetch = 0 if half is None else 1
        arrays = ([] if half is None else [half]) + [a for _, a in ins] + list(filled)
        in_specs = [spec(k, a.shape) for k, a in ins] + [pl.BlockSpec(memory_space=pl.ANY)] * len(filled)
        return pl.pallas_call(
            kernel,
            grid_spec=pltpu.PrefetchScalarGridSpec(
                num_scalar_prefetch=prefetch,
                grid=(steps,),
                in_specs=in_specs,
                out_specs=[spec(k, o.shape) for k, o in outs],
                scratch_shapes=[pltpu.VMEM((r, c if c else columns), t) if r else t for r, c, t in scratch],
            ),
            out_shape=[o for _, o in outs],
            input_output_aliases={prefetch + len(ins) + k: k for k in range(len(filled))},
            compiler_params=pltpu.CompilerParams(vmem_limit_bytes=mib << 20),
            cost_estimate=pl.CostEstimate(
                flops=0, bytes_accessed=int(cost * 3.5e6), transcendentals=0),
        )(*arrays)

    def shaped(self, rows, kind):
        width = self.channels // 2 if kind == "half" else self.channels
        return lambda t: (kind, jax.ShapeDtypeStruct((rows, width), t))

    def small(self):
        return min(8, self.parts // 4)

    def mix(self, half, lengths, v, before, gs, staps, mib):
        out = self.shaped(self.rows, "half")
        return self.call(
            mix_kernel, self.small(), half,
            [("scalars", lengths), ("whole", v), ("whole", before), ("whole", gs), ("whole", staps)],
            [out(BF), out(F32)],
            [(self.rows + RIM, 0, F32), (self.rows, LANES, jnp.int32)], 3, mib)

    def own(self, half, lengths, mixed, adj, ltaps):
        out = self.shaped(self.rows, "half")
        spectrum = (2 * self.rows, 0, F32)
        return self.call(
            own_kernel, self.small(), half,
            [("scalars", lengths), ("half", mixed), ("whole", adj), ("whole", ltaps)]
            + [("table", t) for t in self.tables],
            [out(F32)] * 3,
            [spectrum, spectrum, (0, 0, pltpu.SMEM((16,), jnp.int32))], 1.5, 28)

    def grad(self, half, lengths, v, before, gs, adj, short, back, own_grads, prev, following,
             staps, ltaps, filled):
        first, second, _, front, totaps = self.tables
        rows = self.rows
        out = self.shaped(rows, "whole")
        grads = jax.ShapeDtypeStruct((self.parts // 2, rows + RIM, LANES), BF)
        return self.call(
            grad_kernel, self.small(), half,
            [("scalars", lengths), ("whole", v), ("whole", before), ("whole", gs), ("whole", adj),
             ("half", short), ("half", back), ("half", own_grads), ("half", prev),
             ("whole", following), ("whole", staps), ("whole", ltaps)]
            + [("table", t) for t in (first, second, front, totaps)],
            [out(BF), out(BF), self.shaped(RIM, "whole")(BF), ("shares", grads)],
            [(rows + RIM, 0, F32), (rows, LANES, jnp.int32), (4 * rows, LANES, BF)], 1.5, 28, filled)

    def long(self, half, lengths, gl, up, own_long, prev, ltaps, filled):
        out = self.shaped(self.rows, "whole")
        return self.call(
            long_kernel, self.small(), half,
            [("scalars", lengths), ("whole", gl), ("whole", up), ("half", own_long), ("half", prev),
             ("whole", ltaps), ("table", self.tables[0]), ("table", self.tables[2])],
            [out(BF)] * 2, [(2 * self.rows, LANES, BF)], 3, 56, filled)

    def values_grad(self, lengths, adjs, after, staps):
        return self.call(
            values_kernel, 2 * self.small(), None,
            [("scalars", lengths), ("whole", adjs), ("whole", after), ("whole", staps)],
            [self.shaped(self.rows, "whole")(BF)],
            [(self.count * self.rows, 2 * LANES, BF)], 4, 56)[0]

    def spread(self, mine, other):
        return self.call(
            spread_kernel, self.parts // 2, None, [("table", mine), ("table", other)],
            [self.shaped(self.count, "whole")(F32), self.shaped(self.rows, "whole")(F32)], [], 3, 24)


def traded(block, axes):
    return lax.all_to_all(block, axes, 0, 0, tiled=True)


def copies(block, axes):
    return traded(jnp.broadcast_to(block[None], (lax.axis_size(axes),) + block.shape), axes)


def added(blocks):
    return jnp.sum(blocks.astype(F32), axis=0)


def swapped(block):
    return lax.ppermute(block, "core", [(0, 1), (1, 0)])


def on_device(lengths, values, gate_short, gate_long, short_taps, long_taps, cotangent):
    v, gs, gl, up = values[0], gate_short[0], gate_long[0], cotangent[0]
    rows, channels = v.shape
    k = Kernels(rows, channels, short_taps.shape[0])
    factor = 1.0 / math.sqrt(lax.axis_size(("y", "core", "z", "x")) * rows)
    together = lax.optimization_barrier

    core = lax.axis_index("core").astype(jnp.int32)
    kept = core[None]
    given = 1 - kept

    before = passed_along(v[rows - RIM :], 1)
    adj = (up.astype(F32) * gl.astype(F32)).astype(BF)
    mixed_a, short_a = k.mix(given, lengths, v, before, gs, short_taps, 56)
    mixed_a, adj = together((mixed_a, adj))
    prev_a = passed_along(mixed_a, 1)
    following = passed_along(adj, -1)
    mixed_b, short_b = k.mix(kept, lengths, v, before, gs, short_taps, 20)
    long_a, back_a, terms_a = k.own(given, lengths, mixed_a, adj, long_taps)
    mixed_b, back_a = together((mixed_b, back_a))
    prev_b = passed_along(mixed_b, 1)
    long_b, back_b, terms_b = k.own(kept, lengths, mixed_b, adj, long_taps)
    prev_a, back_b = together((prev_a, back_b))
    ggs, adjs, head, grads_a = k.grad(given, lengths, v, before, gs, adj, short_a, back_a, terms_a,
                                      prev_a, following, short_taps, long_taps, ())
    grads_a, prev_b = together((grads_a, prev_b))
    got = swapped(grads_a)
    ggs, adjs, head, grads_b = k.grad(kept, lengths, v, before, gs, adj, short_b, back_b, terms_b,
                                      prev_b, following, short_taps, long_taps, (ggs, adjs, head))

    planes = ("y", "x")
    half = (grads_b.astype(F32) + got.astype(F32)).astype(BF)
    half, long_a, long_b, head = together((half, long_a, long_b, head))
    share = half.reshape((lax.axis_size(planes), -1) + half.shape[1:])
    share = added(traded(share, planes)).astype(BF)
    after = passed_along(head, -1)
    filled = k.long(given, lengths, gl, up, long_a, prev_a, long_taps, ())
    share, after, filled, long_b = together((share, after, tuple(filled), long_b))
    share = (added(copies(share, "z")) * factor).astype(BF)
    out, ggl = k.long(kept, lengths, gl, up, long_b, prev_b, long_taps, filled)
    share, out, ggl, adjs = together((share, out, ggl, adjs))
    mine = copies(share, planes).reshape(half.shape)
    gv = k.values_grad(lengths, adjs, after, short_taps)
    mine, gv = together((mine, gv))
    grad_short, grad_long = k.spread(mine, swapped(mine))
    return out[None], ggs[None], gv[None], ggl[None], grad_short, grad_long


def solution(mesh):
    dp, ctx = mesh.shape["dp"], mesh.shape["ctx"]
    cut = jax.sharding.Mesh(mesh.devices.reshape(dp // 2, 2, ctx // 4, 4), ("y", "core", "z", "x"))
    rowed = P(("y", "core"), CTX, None)
    return jax.shard_map(
        on_device,
        mesh=cut,
        in_specs=(P(("y", "core"), None), rowed, rowed, rowed, P(), P(), rowed),
        out_specs=(rowed, rowed, rowed, rowed, P(), P()),
        check_vma=False,
    )
```

```python
import math

import jax
import jax.numpy as jnp
import numpy as np
from jax import lax
from jax.experimental import pallas as pl
from jax.experimental.pallas import tpu as pltpu
from jax.sharding import PartitionSpec as P

BF = jnp.bfloat16
F32 = jnp.float32
LANES = 128
RIM = 8
CTX = ("z", "x")


def halves(matrix):
    high = matrix.astype(np.float32).astype(BF)
    low = (matrix - high.astype(np.float64)).astype(np.float32).astype(BF)
    return high, low


def spectra(rows):
    points = 2 * rows
    theta = np.pi * (2 * np.arange(rows) + 1) / points
    angles = theta[:, None] * np.arange(points)[None, :]
    forward = np.concatenate([np.cos(angles), -np.sin(angles)], axis=0)
    inverse = forward.T / rows

    def pack(matrix):
        return np.concatenate(halves(matrix), axis=1)

    def stack(matrix):
        return np.concatenate(halves(matrix), axis=0)

    first = pack(forward[:, :rows])
    second = pack(forward[:, rows:])
    to_later = stack(inverse[rows:])
    to_first = stack(inverse[:rows])
    to_taps = stack(inverse[rows - np.arange(rows)])
    return np.concatenate([first, second, to_later, to_first, to_taps], axis=0)


def matrices(table_ref):
    size = table_ref.shape[1]
    return [lambda at=slice(k * size, (k + 1) * size): table_ref[at, :] for k in range(5)]


def passed_along(block, distance):
    devices = range(lax.axis_size(CTX))
    route = [(i - distance, i) for i in devices if i - distance in devices]
    return lax.ppermute(block, CTX, route)


def wide(row_mask, columns):
    return jnp.concatenate([row_mask] * (columns // LANES), axis=1)


def row_ids(rows):
    return lax.broadcasted_iota(jnp.int32, (rows, LANES), 0)


def cuts_of(lengths_ref, rows):
    at = -lax.axis_index(CTX) * rows
    cuts = [at]
    for d in range(lengths_ref.shape[1]):
        at = at + lengths_ref[0, d]
        cuts.append(at)
    return cuts


def begin_at(cuts, at):
    begin = cuts[0]
    for cut in cuts[1:-1]:
        begin = jnp.where(cut <= at, cut, begin)
    return begin


def end_at(cuts, at):
    end = cuts[-1]
    for cut in cuts[-2:0:-1]:
        end = jnp.where(cut > at, cut, end)
    return end


def times(left, right, conjugate_left):
    half = left.shape[0] // 2
    a, b = left[:half], left[half:]
    c, d = right[:half], right[half:]
    if conjugate_left:
        return jnp.concatenate([a * c + b * d, a * d - b * c], axis=0)
    return jnp.concatenate([a * c - b * d, a * d + b * c], axis=0)


def dot(matrix, data):
    return jnp.dot(matrix, jnp.concatenate([data, data], axis=0), preferred_element_type=F32)


def back_dot(matrix, data):
    both = jnp.dot(matrix, data, preferred_element_type=F32)
    half = matrix.shape[0] // 2
    return both[:half] + both[half:]


def on_first_step(fill):
    pl.when(pl.program_id(0) == 0)(fill)


def mix_kernel(half_ref, lengths_ref, v_ref, before_ref, gs_ref, taps_ref, mixed_ref, short_ref, ext, reach_s):
    rows, columns = v_ref.shape

    @on_first_step
    def _():
        at = row_ids(rows)
        reach_s[...] = at - begin_at(cuts_of(lengths_ref, rows), at)

    ext[0:RIM, :] = before_ref[...].astype(F32)
    ext[RIM:, :] = v_ref[...].astype(F32)
    reach = wide(reach_s[...], columns)
    total = taps_ref[0:1, :] * ext[RIM:, :]
    for j in range(1, taps_ref.shape[0]):
        window = ext[RIM - j : RIM - j + rows, :]
        total = total + taps_ref[j : j + 1, :] * jnp.where(reach >= j, window, 0.0)
    short_ref[...] = total
    mixed_ref[...] = (gs_ref[...].astype(F32) * total).astype(BF)


def note_cuts(lengths_ref, rows, cuts_s):
    low, high = -1, -1
    cuts = cuts_of(lengths_ref, rows)
    for d, cut in enumerate(cuts):
        cuts_s[d] = cut
        if d < len(cuts) - 1:
            low = low + (cut <= 0).astype(jnp.int32)
            high = high + (cut <= rows - 1).astype(jnp.int32)
    return low, high


def own_kernel(half_ref, lengths_ref, mixed_ref, adj_ref, ltaps_ref, table_ref,
               back_ref, grads_ref, taps_spec, spec_acc, cuts_s):
    rows, columns = mixed_ref.shape
    first, second, _, front, totaps = matrices(table_ref)
    low, high = note_cuts(lengths_ref, rows, cuts_s)
    taps_spec[...] = dot(first(), ltaps_ref[...].astype(BF))
    back_ref[...] = jnp.zeros_like(back_ref)
    spec_acc[...] = jnp.zeros_like(spec_acc)
    at = row_ids(rows)

    def document(d, carry):
        inside = jnp.where((at >= cuts_s[d]) & (at < cuts_s[d + 1]), 1.0, 0.0)
        own_bf = wide(inside.astype(BF), columns)
        x_spec = dot(second(), mixed_ref[...] * own_bf)
        a_spec = dot(first(), adj_ref[...] * own_bf)
        spec_acc[...] += times(a_spec, x_spec, True)
        product = times(taps_spec[...], a_spec, True).astype(BF)
        back_ref[...] += wide(inside, columns) * back_dot(front(), product)
        return carry

    lax.fori_loop(low, high + 1, document, 0)
    grads_ref[...] = back_dot(totaps(), spec_acc[...].astype(BF))


def grad_kernel(half_ref, lengths_ref, v_ref, before_ref, gs_ref, adj_ref, short_ref, back_ref, own_grads_ref,
                prev_ref, next_ref, staps_ref, ltaps_ref, table_ref, *rest):
    ggs_ref, adjs_ref, head_ref, grads_ref, ext, reach_s, masks_s = rest[-7:]
    rows, columns = v_ref.shape
    first, second, _, front, totaps = matrices(table_ref)

    @on_first_step
    def _():
        at = row_ids(rows)
        cuts = cuts_of(lengths_ref, rows)
        reach_s[...] = at - begin_at(cuts, at)
        ones = lambda mask: jnp.where(mask, 1.0, 0.0).astype(BF)
        masks_s[0 * rows : 1 * rows, :] = ones(at < end_at(cuts, 0))
        masks_s[1 * rows : 2 * rows, :] = ones(at - rows >= begin_at(cuts, 0))
        masks_s[2 * rows : 3 * rows, :] = ones(at >= begin_at(cuts, rows - 1))
        masks_s[3 * rows : 4 * rows, :] = ones(at + rows < end_at(cuts, rows - 1))

    mask = lambda k: wide(masks_s[k * rows : (k + 1) * rows, :], columns)
    taps_spec = dot(first(), ltaps_ref[...].astype(BF))
    next_spec = dot(second(), next_ref[...] * mask(3))
    product = times(taps_spec, next_spec, True).astype(BF)
    back = back_ref[...] + mask(2).astype(F32) * back_dot(front(), product)
    prev_spec = dot(first(), prev_ref[...] * mask(1))
    own_spec = dot(first(), adj_ref[...] * mask(0))
    product = times(own_spec, prev_spec, True).astype(BF)
    long_terms = own_grads_ref[...] + back_dot(totaps(), product)

    ggs_ref[...] = (back * short_ref[...]).astype(BF)
    adj_short = (back * gs_ref[...].astype(F32)).astype(BF)
    adjs_ref[...] = adj_short
    adj_short = adj_short.astype(F32)
    head_ref[...] = adj_short[0:RIM].astype(BF)
    ext[0:RIM, :] = before_ref[...].astype(F32)
    ext[RIM:, :] = v_ref[...].astype(F32)
    reach = wide(reach_s[...], columns)
    terms = [jnp.sum(adj_short * ext[RIM:, :], axis=0, keepdims=True)]
    for j in range(1, staps_ref.shape[0]):
        window = ext[RIM - j : RIM - j + rows, :]
        terms.append(jnp.sum(jnp.where(reach >= j, adj_short * window, 0.0), axis=0, keepdims=True))
    terms.append(jnp.zeros((RIM - len(terms), columns), F32))
    terms = jnp.concatenate([long_terms] + terms, axis=0).astype(BF)
    for k in range(columns // LANES):
        grads_ref[k] = terms[:, k * LANES : (k + 1) * LANES]


def long_kernel(half_ref, lengths_ref, gl_ref, up_ref, mixed_ref, prev_ref, ltaps_ref, table_ref, *rest):
    out_ref, ggl_ref, taps_spec, prev_spec, long_acc, cuts_s = rest[-6:]
    rows, columns = gl_ref.shape
    first, second, later, _, _ = matrices(table_ref)
    low, high = note_cuts(lengths_ref, rows, cuts_s)
    at = row_ids(rows)
    earlier = jnp.where(at - rows >= cuts_s[low], 1.0, 0.0).astype(BF)
    taps_spec[...] = dot(first(), ltaps_ref[...].astype(BF))
    prev_spec[...] = dot(first(), prev_ref[...] * wide(earlier, columns))
    long_acc[...] = jnp.zeros_like(long_acc)

    def document(d, carry):
        inside = jnp.where((at >= cuts_s[d]) & (at < cuts_s[d + 1]), 1.0, 0.0)
        reaches_back = jnp.where(d == low, 1.0, 0.0)
        x_spec = dot(second(), mixed_ref[...] * wide(inside.astype(BF), columns))
        x_spec = x_spec + reaches_back * prev_spec[...]
        product = times(taps_spec[...], x_spec, False).astype(BF)
        long_acc[...] += wide(inside, columns) * back_dot(later(), product)
        return carry

    lax.fori_loop(low, high + 1, document, 0)
    long_mix = long_acc[...]
    out_ref[...] = (gl_ref[...].astype(F32) * long_mix).astype(BF)
    ggl_ref[...] = (up_ref[...].astype(F32) * long_mix).astype(BF)


def values_kernel(lengths_ref, adjs_ref, after_ref, taps_ref, gv_ref, move):
    rows, columns = adjs_ref.shape
    count = taps_ref.shape[0]

    @on_first_step
    def _():
        at = lax.broadcasted_iota(jnp.int32, (rows, 2 * LANES), 0)
        source = lax.broadcasted_iota(jnp.int32, (rows, 2 * LANES), 1)
        left = end_at(cuts_of(lengths_ref, rows), at) - at
        for j in range(count):
            move[j * rows : (j + 1) * rows, :] = jnp.where(
                (source == at + j) & (left > j), 1.0, 0.0).astype(BF)

    rim = jnp.concatenate([after_ref[...].astype(F32), jnp.zeros((LANES - RIM, columns), F32)], axis=0)
    data = jnp.concatenate([adjs_ref[...], rim.astype(BF)], axis=0)
    moved = jnp.dot(move[...], data, preferred_element_type=F32)
    total = taps_ref[0:1, :] * moved[:rows]
    for j in range(1, count):
        total = total + taps_ref[j : j + 1, :] * moved[j * rows : (j + 1) * rows]
    gv_ref[...] = total.astype(BF)


def spread_kernel(mine_ref, other_ref, short_ref, long_ref):
    rows = long_ref.shape[0]

    def write(blocks):
        for k in range(blocks.shape[0]):
            shares = blocks[k].astype(F32)
            at = slice(k * LANES, (k + 1) * LANES)
            long_ref[:, at] = shares[:rows]
            short_ref[:, at] = shares[rows : rows + short_ref.shape[0]]

    own_turn = pl.program_id(0) == lax.axis_index("core")
    pl.when(own_turn)(lambda: write(mine_ref))
    pl.when(jnp.logical_not(own_turn))(lambda: write(other_ref))


class Kernels:

    def __init__(self, rows, channels, count):
        self.rows, self.channels, self.count = rows, channels, count
        self.parts = channels // LANES
        self.table = jnp.asarray(spectra(rows))

    def call(self, kernel, step_parts, half, ins, outs, scratch, cost, mib, filled=()):
        columns = step_parts * LANES
        steps = self.parts // step_parts
        if half is not None:
            steps //= 2

        def spec(kind, shape):
            if kind == "scalars":
                return pl.BlockSpec(memory_space=pltpu.SMEM)
            if kind == "table":
                return pl.BlockSpec(shape, lambda i, *h: (0,) * len(shape))
            if kind == "shares":
                return pl.BlockSpec((step_parts,) + shape[1:], lambda i, *h: (i, 0, 0))
            if kind == "whole" and half is not None:
                return pl.BlockSpec((shape[0], columns), lambda i, h: (0, h[0] * steps + i))
            return pl.BlockSpec((shape[0], columns), lambda i, *h: (0, i))

        prefetch = 0 if half is None else 1
        arrays = ([] if half is None else [half]) + [a for _, a in ins] + list(filled)
        in_specs = [spec(k, a.shape) for k, a in ins] + [pl.BlockSpec(memory_space=pl.ANY)] * len(filled)
        return pl.pallas_call(
            kernel,
            grid_spec=pltpu.PrefetchScalarGridSpec(
                num_scalar_prefetch=prefetch,
                grid=(steps,),
                in_specs=in_specs,
                out_specs=[spec(k, o.shape) for k, o in outs],
                scratch_shapes=[pltpu.VMEM((r, c if c else columns), t) if r else t for r, c, t in scratch],
            ),
            out_shape=[o for _, o in outs],
            input_output_aliases={prefetch + len(ins) + k: k for k in range(len(filled))},
            compiler_params=pltpu.CompilerParams(vmem_limit_bytes=mib << 20),
            cost_estimate=pl.CostEstimate(
                flops=0, bytes_accessed=int(cost * 3.5e6), transcendentals=0),
        )(*arrays)

    def shaped(self, rows, kind):
        width = self.channels // 2 if kind == "half" else self.channels
        return lambda t: (kind, jax.ShapeDtypeStruct((rows, width), t))

    def small(self):
        return min(8, self.parts // 4)

    def mix(self, half, lengths, v, before, gs, staps, mib):
        out = self.shaped(self.rows, "half")
        return self.call(
            mix_kernel, self.small(), half,
            [("scalars", lengths), ("whole", v), ("whole", before), ("whole", gs), ("whole", staps)],
            [out(BF), out(F32)],
            [(self.rows + RIM, 0, F32), (self.rows, LANES, jnp.int32)], 3, mib)

    def own(self, half, lengths, mixed, adj, ltaps):
        out = self.shaped(self.rows, "half")
        spectrum = (2 * self.rows, 0, F32)
        return self.call(
            own_kernel, self.small(), half,
            [("scalars", lengths), ("half", mixed), ("whole", adj), ("whole", ltaps),
             ("table", self.table)],
            [out(F32)] * 2,
            [spectrum, spectrum, (0, 0, pltpu.SMEM((16,), jnp.int32))], 1.5, 28)

    def grad(self, half, lengths, v, before, gs, adj, short, back, own_grads, prev, following,
             staps, ltaps, filled):
        rows = self.rows
        out = self.shaped(rows, "whole")
        grads = jax.ShapeDtypeStruct((self.parts // 2, rows + RIM, LANES), BF)
        return self.call(
            grad_kernel, self.small(), half,
            [("scalars", lengths), ("whole", v), ("whole", before), ("whole", gs), ("whole", adj),
             ("half", short), ("half", back), ("half", own_grads), ("half", prev),
             ("whole", following), ("whole", staps), ("whole", ltaps), ("table", self.table)],
            [out(BF), out(BF), self.shaped(RIM, "whole")(BF), ("shares", grads)],
            [(rows + RIM, 0, F32), (rows, LANES, jnp.int32), (4 * rows, LANES, BF)], 1.5, 28, filled)

    def long(self, half, lengths, gl, up, mixed, prev, ltaps, filled):
        out = self.shaped(self.rows, "whole")
        spectrum = (2 * self.rows, 0, F32)
        return self.call(
            long_kernel, self.small(), half,
            [("scalars", lengths), ("whole", gl), ("whole", up), ("half", mixed), ("half", prev),
             ("whole", ltaps), ("table", self.table)],
            [out(BF)] * 2,
            [spectrum, spectrum, (self.rows, 0, F32), (0, 0, pltpu.SMEM((16,), jnp.int32))], 3, 56, filled)

    def values_grad(self, lengths, adjs, after, staps):
        return self.call(
            values_kernel, 2 * self.small(), None,
            [("scalars", lengths), ("whole", adjs), ("whole", after), ("whole", staps)],
            [self.shaped(self.rows, "whole")(BF)],
            [(self.count * self.rows, 2 * LANES, BF)], 4, 56)[0]

    def spread(self, mine, other):
        return self.call(
            spread_kernel, self.parts // 2, None, [("table", mine), ("table", other)],
            [self.shaped(self.count, "whole")(F32), self.shaped(self.rows, "whole")(F32)], [], 3, 24)


def traded(block, axes):
    return lax.all_to_all(block, axes, 0, 0, tiled=True)


def copies(block, axes):
    return traded(jnp.broadcast_to(block[None], (lax.axis_size(axes),) + block.shape), axes)


def added(blocks):
    return jnp.sum(blocks.astype(F32), axis=0)


def swapped(block):
    return lax.ppermute(block, "core", [(0, 1), (1, 0)])


def on_device(lengths, values, gate_short, gate_long, short_taps, long_taps, cotangent):
    v, gs, gl, up = values[0], gate_short[0], gate_long[0], cotangent[0]
    rows, channels = v.shape
    k = Kernels(rows, channels, short_taps.shape[0])
    factor = 1.0 / math.sqrt(lax.axis_size(("y", "core", "z", "x")) * rows)
    together = lax.optimization_barrier

    core = lax.axis_index("core").astype(jnp.int32)
    kept = core[None]
    given = 1 - kept

    before = passed_along(v[rows - RIM :], 1)
    adj = (up.astype(F32) * gl.astype(F32)).astype(BF)
    mixed_a, short_a = k.mix(given, lengths, v, before, gs, short_taps, 56)
    mixed_a, adj = together((mixed_a, adj))
    prev_a = passed_along(mixed_a, 1)
    following = passed_along(adj, -1)
    mixed_b, short_b = k.mix(kept, lengths, v, before, gs, short_taps, 20)
    back_a, terms_a = k.own(given, lengths, mixed_a, adj, long_taps)
    mixed_b, back_a = together((mixed_b, back_a))
    prev_b = passed_along(mixed_b, 1)
    back_b, terms_b = k.own(kept, lengths, mixed_b, adj, long_taps)
    prev_a, back_b = together((prev_a, back_b))
    ggs, adjs, head, grads_a = k.grad(given, lengths, v, before, gs, adj, short_a, back_a, terms_a,
                                      prev_a, following, short_taps, long_taps, ())
    grads_a, prev_b = together((grads_a, prev_b))
    got = swapped(grads_a)
    ggs, adjs, head, grads_b = k.grad(kept, lengths, v, before, gs, adj, short_b, back_b, terms_b,
                                      prev_b, following, short_taps, long_taps, (ggs, adjs, head))

    planes = ("y", "x")
    half = (grads_b.astype(F32) + got.astype(F32)).astype(BF)
    half, mixed_a, mixed_b, head = together((half, mixed_a, mixed_b, head))
    share = half.reshape((lax.axis_size(planes), -1) + half.shape[1:])
    share = added(traded(share, planes)).astype(BF)
    after = passed_along(head, -1)
    filled = k.long(given, lengths, gl, up, mixed_a, prev_a, long_taps, ())
    share, after, filled, mixed_b = together((share, after, tuple(filled), mixed_b))
    share = (added(copies(share, "z")) * factor).astype(BF)
    out, ggl = k.long(kept, lengths, gl, up, mixed_b, prev_b, long_taps, filled)
    share, out, ggl, adjs = together((share, out, ggl, adjs))
    mine = copies(share, planes).reshape(half.shape)
    gv = k.values_grad(lengths, adjs, after, short_taps)
    mine, gv = together((mine, gv))
    grad_short, grad_long = k.spread(mine, swapped(mine))
    return out[None], ggs[None], gv[None], ggl[None], grad_short, grad_long


def solution(mesh):
    dp, ctx = mesh.shape["dp"], mesh.shape["ctx"]
    cut = jax.sharding.Mesh(mesh.devices.reshape(dp // 2, 2, ctx // 4, 4), ("y", "core", "z", "x"))
    rowed = P(("y", "core"), CTX, None)
    return jax.shard_map(
        on_device,
        mesh=cut,
        in_specs=(P(("y", "core"), None), rowed, rowed, rowed, P(), P(), rowed),
        out_specs=(rowed, rowed, rowed, rowed, P(), P()),
        check_vma=False,
    )
```

```python
import math

import jax
import jax.numpy as jnp
import numpy as np
from jax import lax
from jax.experimental import pallas as pl
from jax.experimental.pallas import tpu as pltpu
from jax.sharding import PartitionSpec as P

BF = jnp.bfloat16
F32 = jnp.float32
LANES = 128
RIM = 8
CTX = ("z", "x")


def halves(matrix):
    high = matrix.astype(np.float32).astype(BF)
    low = (matrix - high.astype(np.float64)).astype(np.float32).astype(BF)
    return high, low


def spectra(rows):
    points = 2 * rows
    theta = np.pi * (2 * np.arange(rows) + 1) / points
    angles = theta[:, None] * np.arange(points)[None, :]
    forward = np.concatenate([np.cos(angles), -np.sin(angles)], axis=0)
    inverse = forward.T / rows

    def pack(matrix):
        return np.concatenate(halves(matrix), axis=1)

    def stack(matrix):
        return np.concatenate(halves(matrix), axis=0)

    first = pack(forward[:, :rows])
    second = pack(forward[:, rows:])
    to_later = stack(inverse[rows:])
    to_first = stack(inverse[:rows])
    to_taps = stack(inverse[rows - np.arange(rows)])
    return np.concatenate([first, second, to_later, to_first, to_taps], axis=0)


def matrices(table_ref):
    size = table_ref.shape[1]
    return [lambda at=slice(k * size, (k + 1) * size): table_ref[at, :] for k in range(5)]


def passed_along(block, distance):
    devices = range(lax.axis_size(CTX))
    route = [(i - distance, i) for i in devices if i - distance in devices]
    return lax.ppermute(block, CTX, route)


def wide(row_mask, columns):
    return jnp.concatenate([row_mask] * (columns // LANES), axis=1)


def row_ids(rows):
    return lax.broadcasted_iota(jnp.int32, (rows, LANES), 0)


def cuts_of(lengths_ref, rows):
    at = -lax.axis_index(CTX) * rows
    cuts = [at]
    for d in range(lengths_ref.shape[1]):
        at = at + lengths_ref[0, d]
        cuts.append(at)
    return cuts


def begin_at(cuts, at):
    begin = cuts[0]
    for cut in cuts[1:-1]:
        begin = jnp.where(cut <= at, cut, begin)
    return begin


def end_at(cuts, at):
    end = cuts[-1]
    for cut in cuts[-2:0:-1]:
        end = jnp.where(cut > at, cut, end)
    return end


def times(left, right, conjugate_left):
    half = left.shape[0] // 2
    a, b = left[:half], left[half:]
    c, d = right[:half], right[half:]
    if conjugate_left:
        return jnp.concatenate([a * c + b * d, a * d - b * c], axis=0)
    return jnp.concatenate([a * c - b * d, a * d + b * c], axis=0)


def dot(matrix, data):
    return jnp.dot(matrix, jnp.concatenate([data, data], axis=0), preferred_element_type=F32)


def back_dot(matrix, data):
    both = jnp.dot(matrix, data, preferred_element_type=F32)
    half = matrix.shape[0] // 2
    return both[:half] + both[half:]


def on_first_step(fill):
    pl.when(pl.program_id(0) == 0)(fill)


def mix_kernel(half_ref, lengths_ref, v_ref, before_ref, gs_ref, taps_ref, mixed_ref, short_ref, ext, reach_s):
    rows, columns = v_ref.shape

    @on_first_step
    def _():
        at = row_ids(rows)
        reach_s[...] = at - begin_at(cuts_of(lengths_ref, rows), at)

    ext[0:RIM, :] = before_ref[...].astype(F32)
    ext[RIM:, :] = v_ref[...].astype(F32)
    reach = wide(reach_s[...], columns)
    total = taps_ref[0:1, :] * ext[RIM:, :]
    for j in range(1, taps_ref.shape[0]):
        window = ext[RIM - j : RIM - j + rows, :]
        total = total + taps_ref[j : j + 1, :] * jnp.where(reach >= j, window, 0.0)
    short_ref[...] = total
    mixed_ref[...] = (gs_ref[...].astype(F32) * total).astype(BF)


def note_cuts(lengths_ref, rows, cuts_s):
    low, high = -1, -1
    cuts = cuts_of(lengths_ref, rows)
    for d, cut in enumerate(cuts):
        cuts_s[d] = cut
        if d < len(cuts) - 1:
            low = low + (cut <= 0).astype(jnp.int32)
            high = high + (cut <= rows - 1).astype(jnp.int32)
    return low, high


def own_kernel(half_ref, lengths_ref, mixed_ref, adj_ref, ltaps_ref, table_ref,
               back_ref, grads_ref, taps_spec, spec_acc, cuts_s):
    rows, columns = mixed_ref.shape
    first, second, _, front, totaps = matrices(table_ref)
    low, high = note_cuts(lengths_ref, rows, cuts_s)
    taps_spec[...] = dot(first(), ltaps_ref[...].astype(BF))
    back_ref[...] = jnp.zeros_like(back_ref)
    spec_acc[...] = jnp.zeros_like(spec_acc)
    at = row_ids(rows)

    def document(d, carry):
        inside = jnp.where((at >= cuts_s[d]) & (at < cuts_s[d + 1]), 1.0, 0.0)
        own_bf = wide(inside.astype(BF), columns)
        x_spec = dot(second(), mixed_ref[...] * own_bf)
        a_spec = dot(first(), adj_ref[...] * own_bf)
        spec_acc[...] += times(a_spec, x_spec, True)
        product = times(taps_spec[...], a_spec, True).astype(BF)
        back_ref[...] += wide(inside, columns) * back_dot(front(), product)
        return carry

    lax.fori_loop(low, high + 1, document, 0)
    grads_ref[...] = back_dot(totaps(), spec_acc[...].astype(BF))


def grad_kernel(half_ref, lengths_ref, v_ref, before_ref, gs_ref, adj_ref, short_ref, back_ref, own_grads_ref,
                prev_ref, next_ref, staps_ref, ltaps_ref, table_ref, *rest):
    ggs_ref, adjs_ref, head_ref, grads_ref, ext, reach_s, masks_s = rest[-7:]
    rows, columns = v_ref.shape
    first, second, _, front, totaps = matrices(table_ref)

    @on_first_step
    def _():
        at = row_ids(rows)
        cuts = cuts_of(lengths_ref, rows)
        reach_s[...] = at - begin_at(cuts, at)
        ones = lambda mask: jnp.where(mask, 1.0, 0.0).astype(BF)
        masks_s[0 * rows : 1 * rows, :] = ones(at < end_at(cuts, 0))
        masks_s[1 * rows : 2 * rows, :] = ones(at - rows >= begin_at(cuts, 0))
        masks_s[2 * rows : 3 * rows, :] = ones(at >= begin_at(cuts, rows - 1))
        masks_s[3 * rows : 4 * rows, :] = ones(at + rows < end_at(cuts, rows - 1))

    mask = lambda k: wide(masks_s[k * rows : (k + 1) * rows, :], columns)
    taps_spec = dot(first(), ltaps_ref[...].astype(BF))
    next_spec = dot(second(), next_ref[...] * mask(3))
    product = times(taps_spec, next_spec, True).astype(BF)
    back = back_ref[...] + mask(2).astype(F32) * back_dot(front(), product)
    prev_spec = dot(first(), prev_ref[...] * mask(1))
    own_spec = dot(first(), adj_ref[...] * mask(0))
    product = times(own_spec, prev_spec, True).astype(BF)
    long_terms = own_grads_ref[...] + back_dot(totaps(), product)

    ggs_ref[...] = (back * short_ref[...]).astype(BF)
    adj_short = (back * gs_ref[...].astype(F32)).astype(BF)
    adjs_ref[...] = adj_short
    adj_short = adj_short.astype(F32)
    head_ref[...] = adj_short[0:RIM].astype(BF)
    ext[0:RIM, :] = before_ref[...].astype(F32)
    ext[RIM:, :] = v_ref[...].astype(F32)
    reach = wide(reach_s[...], columns)
    terms = [jnp.sum(adj_short * ext[RIM:, :], axis=0, keepdims=True)]
    for j in range(1, staps_ref.shape[0]):
        window = ext[RIM - j : RIM - j + rows, :]
        terms.append(jnp.sum(jnp.where(reach >= j, adj_short * window, 0.0), axis=0, keepdims=True))
    terms.append(jnp.zeros((RIM - len(terms), columns), F32))
    terms = jnp.concatenate([long_terms] + terms, axis=0).astype(BF)
    for k in range(columns // LANES):
        grads_ref[k] = terms[:, k * LANES : (k + 1) * LANES]


def long_kernel(half_ref, lengths_ref, gl_ref, up_ref, mixed_ref, prev_ref, ltaps_ref, table_ref, *rest):
    out_ref, ggl_ref, taps_spec, prev_spec, long_acc, cuts_s = rest[-6:]
    rows, columns = gl_ref.shape
    first, second, later, _, _ = matrices(table_ref)
    low, high = note_cuts(lengths_ref, rows, cuts_s)
    at = row_ids(rows)
    earlier = jnp.where(at - rows >= cuts_s[low], 1.0, 0.0).astype(BF)
    taps_spec[...] = dot(first(), ltaps_ref[...].astype(BF))
    prev_spec[...] = dot(first(), prev_ref[...] * wide(earlier, columns))
    long_acc[...] = jnp.zeros_like(long_acc)

    def document(d, carry):
        inside = jnp.where((at >= cuts_s[d]) & (at < cuts_s[d + 1]), 1.0, 0.0)
        reaches_back = jnp.where(d == low, 1.0, 0.0)
        x_spec = dot(second(), mixed_ref[...] * wide(inside.astype(BF), columns))
        x_spec = x_spec + reaches_back * prev_spec[...]
        product = times(taps_spec[...], x_spec, False).astype(BF)
        long_acc[...] += wide(inside, columns) * back_dot(later(), product)
        return carry

    lax.fori_loop(low, high + 1, document, 0)
    long_mix = long_acc[...]
    out_ref[...] = (gl_ref[...].astype(F32) * long_mix).astype(BF)
    ggl_ref[...] = (up_ref[...].astype(F32) * long_mix).astype(BF)


def values_kernel(lengths_ref, adjs_ref, after_ref, taps_ref, gv_ref, move):
    rows, columns = adjs_ref.shape
    count = taps_ref.shape[0]

    @on_first_step
    def _():
        at = lax.broadcasted_iota(jnp.int32, (rows, 2 * LANES), 0)
        source = lax.broadcasted_iota(jnp.int32, (rows, 2 * LANES), 1)
        left = end_at(cuts_of(lengths_ref, rows), at) - at
        for j in range(count):
            move[j * rows : (j + 1) * rows, :] = jnp.where(
                (source == at + j) & (left > j), 1.0, 0.0).astype(BF)

    rim = jnp.concatenate([after_ref[...].astype(F32), jnp.zeros((LANES - RIM, columns), F32)], axis=0)
    data = jnp.concatenate([adjs_ref[...], rim.astype(BF)], axis=0)
    moved = jnp.dot(move[...], data, preferred_element_type=F32)
    total = taps_ref[0:1, :] * moved[:rows]
    for j in range(1, count):
        total = total + taps_ref[j : j + 1, :] * moved[j * rows : (j + 1) * rows]
    gv_ref[...] = total.astype(BF)


def spread_kernel(mine_ref, other_ref, short_ref, long_ref):
    rows = long_ref.shape[0]

    def write(blocks):
        for k in range(blocks.shape[0]):
            shares = blocks[k].astype(F32)
            at = slice(k * LANES, (k + 1) * LANES)
            long_ref[:, at] = shares[:rows]
            short_ref[:, at] = shares[rows : rows + short_ref.shape[0]]

    own_turn = pl.program_id(0) == lax.axis_index("core")
    pl.when(own_turn)(lambda: write(mine_ref))
    pl.when(jnp.logical_not(own_turn))(lambda: write(other_ref))


class Kernels:

    def __init__(self, rows, channels, count):
        self.rows, self.channels, self.count = rows, channels, count
        self.parts = channels // LANES
        self.table = jnp.asarray(spectra(rows))

    def call(self, kernel, step_parts, half, ins, outs, scratch, cost, mib, filled=()):
        columns = step_parts * LANES
        steps = self.parts // step_parts
        if half is not None:
            steps //= 2

        def spec(kind, shape):
            if kind == "scalars":
                return pl.BlockSpec(memory_space=pltpu.SMEM)
            if kind == "table":
                return pl.BlockSpec(shape, lambda i, *h: (0,) * len(shape))
            if kind == "shares":
                return pl.BlockSpec((step_parts,) + shape[1:], lambda i, *h: (i, 0, 0))
            if kind == "whole" and half is not None:
                return pl.BlockSpec((shape[0], columns), lambda i, h: (0, h[0] * steps + i))
            return pl.BlockSpec((shape[0], columns), lambda i, *h: (0, i))

        prefetch = 0 if half is None else 1
        arrays = ([] if half is None else [half]) + [a for _, a in ins] + list(filled)
        in_specs = [spec(k, a.shape) for k, a in ins] + [pl.BlockSpec(memory_space=pl.ANY)] * len(filled)
        return pl.pallas_call(
            kernel,
            grid_spec=pltpu.PrefetchScalarGridSpec(
                num_scalar_prefetch=prefetch,
                grid=(steps,),
                in_specs=in_specs,
                out_specs=[spec(k, o.shape) for k, o in outs],
                scratch_shapes=[pltpu.VMEM((r, c if c else columns), t) if r else t for r, c, t in scratch],
            ),
            out_shape=[o for _, o in outs],
            input_output_aliases={prefetch + len(ins) + k: k for k in range(len(filled))},
            compiler_params=pltpu.CompilerParams(vmem_limit_bytes=mib << 20),
            cost_estimate=pl.CostEstimate(
                flops=0, bytes_accessed=int(cost * 3.5e6), transcendentals=0),
        )(*arrays)

    def shaped(self, rows, kind):
        width = self.channels // 2 if kind == "half" else self.channels
        return lambda t: (kind, jax.ShapeDtypeStruct((rows, width), t))

    def small(self):
        return min(8, self.parts // 4)

    def mix(self, half, lengths, v, before, gs, staps, mib):
        out = self.shaped(self.rows, "half")
        return self.call(
            mix_kernel, self.small(), half,
            [("scalars", lengths), ("whole", v), ("whole", before), ("whole", gs), ("whole", staps)],
            [out(BF), out(F32)],
            [(self.rows + RIM, 0, F32), (self.rows, LANES, jnp.int32)], 3, mib)

    def own(self, half, lengths, mixed, adj, ltaps):
        out = self.shaped(self.rows, "half")
        spectrum = (2 * self.rows, 0, F32)
        return self.call(
            own_kernel, self.small(), half,
            [("scalars", lengths), ("half", mixed), ("whole", adj), ("whole", ltaps),
             ("table", self.table)],
            [out(F32)] * 2,
            [spectrum, spectrum, (0, 0, pltpu.SMEM((16,), jnp.int32))], 1.5, 28)

    def grad(self, half, lengths, v, before, gs, adj, short, back, own_grads, prev, following,
             staps, ltaps, filled):
        rows = self.rows
        out = self.shaped(rows, "whole")
        grads = jax.ShapeDtypeStruct((self.parts // 2, rows + RIM, LANES), BF)
        return self.call(
            grad_kernel, self.small(), half,
            [("scalars", lengths), ("whole", v), ("whole", before), ("whole", gs), ("whole", adj),
             ("half", short), ("half", back), ("half", own_grads), ("half", prev),
             ("whole", following), ("whole", staps), ("whole", ltaps), ("table", self.table)],
            [out(BF), out(BF), self.shaped(RIM, "whole")(BF), ("shares", grads)],
            [(rows + RIM, 0, F32), (rows, LANES, jnp.int32), (4 * rows, LANES, BF)], 1.5, 28, filled)

    def long(self, half, lengths, gl, up, mixed, prev, ltaps, filled):
        out = self.shaped(self.rows, "whole")
        spectrum = (2 * self.rows, 0, F32)
        return self.call(
            long_kernel, self.small(), half,
            [("scalars", lengths), ("whole", gl), ("whole", up), ("half", mixed), ("half", prev),
             ("whole", ltaps), ("table", self.table)],
            [out(BF)] * 2,
            [spectrum, spectrum, (self.rows, 0, F32), (0, 0, pltpu.SMEM((16,), jnp.int32))], 3, 56, filled)

    def values_grad(self, lengths, adjs, after, staps):
        return self.call(
            values_kernel, 2 * self.small(), None,
            [("scalars", lengths), ("whole", adjs), ("whole", after), ("whole", staps)],
            [self.shaped(self.rows, "whole")(BF)],
            [(self.count * self.rows, 2 * LANES, BF)], 4, 56)[0]

    def spread(self, mine, other):
        return self.call(
            spread_kernel, self.parts // 2, None, [("table", mine), ("table", other)],
            [self.shaped(self.count, "whole")(F32), self.shaped(self.rows, "whole")(F32)], [], 3, 24)


def traded(block, axes):
    return lax.all_to_all(block, axes, 0, 0, tiled=True)


def copies(block, axes):
    return traded(jnp.broadcast_to(block[None], (lax.axis_size(axes),) + block.shape), axes)


def added(blocks):
    return jnp.sum(blocks.astype(F32), axis=0)


def swapped(block):
    return lax.ppermute(block, "core", [(0, 1), (1, 0)])


def on_device(lengths, values, gate_short, gate_long, short_taps, long_taps, cotangent):
    v, gs, gl, up = values[0], gate_short[0], gate_long[0], cotangent[0]
    rows, channels = v.shape
    k = Kernels(rows, channels, short_taps.shape[0])
    factor = 1.0 / math.sqrt(lax.axis_size(("y", "core", "z", "x")) * rows)
    together = lax.optimization_barrier

    core = lax.axis_index("core").astype(jnp.int32)
    kept = core[None]
    given = 1 - kept

    before = passed_along(v[rows - RIM :], 1)
    adj = (up.astype(F32) * gl.astype(F32)).astype(BF)
    before, adj = together((before, adj))
    following = passed_along(adj, -1)
    mixed_a, short_a = k.mix(given, lengths, v, before, gs, short_taps, 56)
    prev_a = passed_along(mixed_a, 1)
    back_a, terms_a = k.own(given, lengths, mixed_a, adj, long_taps)
    before, back_a = together((before, back_a))
    mixed_b, short_b = k.mix(kept, lengths, v, before, gs, short_taps, 20)
    prev_b = passed_along(mixed_b, 1)
    back_b, terms_b = k.own(kept, lengths, mixed_b, adj, long_taps)
    prev_a, back_b = together((prev_a, back_b))
    ggs, adjs, head, grads_a = k.grad(given, lengths, v, before, gs, adj, short_a, back_a, terms_a,
                                      prev_a, following, short_taps, long_taps, ())
    grads_a, prev_b = together((grads_a, prev_b))
    got = swapped(grads_a)
    ggs, adjs, head, grads_b = k.grad(kept, lengths, v, before, gs, adj, short_b, back_b, terms_b,
                                      prev_b, following, short_taps, long_taps, (ggs, adjs, head))

    planes = ("y", "x")
    half = (grads_b.astype(F32) + got.astype(F32)).astype(BF)
    half, mixed_a, mixed_b, head = together((half, mixed_a, mixed_b, head))
    share = half.reshape((lax.axis_size(planes), -1) + half.shape[1:])
    share = added(traded(share, planes)).astype(BF)
    after = passed_along(head, -1)
    filled = k.long(given, lengths, gl, up, mixed_a, prev_a, long_taps, ())
    share, after, filled, mixed_b = together((share, after, tuple(filled), mixed_b))
    share = (added(copies(share, "z")) * factor).astype(BF)
    out, ggl = k.long(kept, lengths, gl, up, mixed_b, prev_b, long_taps, filled)
    share, out, ggl, adjs = together((share, out, ggl, adjs))
    mine = copies(share, planes).reshape(half.shape)
    gv = k.values_grad(lengths, adjs, after, short_taps)
    mine, gv = together((mine, gv))
    grad_short, grad_long = k.spread(mine, swapped(mine))
    return out[None], ggs[None], gv[None], ggl[None], grad_short, grad_long


def solution(mesh):
    dp, ctx = mesh.shape["dp"], mesh.shape["ctx"]
    cut = jax.sharding.Mesh(mesh.devices.reshape(dp // 2, 2, ctx // 4, 4), ("y", "core", "z", "x"))
    rowed = P(("y", "core"), CTX, None)
    return jax.shard_map(
        on_device,
        mesh=cut,
        in_specs=(P(("y", "core"), None), rowed, rowed, rowed, P(), P(), rowed),
        out_specs=(rowed, rowed, rowed, rowed, P(), P()),
        check_vma=False,
    )
```

```python
import math

import jax
import jax.numpy as jnp
import numpy as np
from jax import lax
from jax.experimental import pallas as pl
from jax.experimental.pallas import tpu as pltpu
from jax.sharding import PartitionSpec as P

BF = jnp.bfloat16
F32 = jnp.float32
LANES = 128
RIM = 8
CTX = ("z", "x")


def halves(matrix):
    high = matrix.astype(np.float32).astype(BF)
    low = (matrix - high.astype(np.float64)).astype(np.float32).astype(BF)
    return high, low


def spectra(rows):
    points = 2 * rows
    theta = np.pi * (2 * np.arange(rows) + 1) / points
    angles = theta[:, None] * np.arange(points)[None, :]
    forward = np.concatenate([np.cos(angles), -np.sin(angles)], axis=0)
    inverse = forward.T / rows

    def pack(matrix):
        return np.concatenate(halves(matrix), axis=1)

    def stack(matrix):
        return np.concatenate(halves(matrix), axis=0)

    first = pack(forward[:, :rows])
    second = pack(forward[:, rows:])
    to_later = stack(inverse[rows:])
    to_first = stack(inverse[:rows])
    to_taps = stack(inverse[rows - np.arange(rows)])
    return np.concatenate([first, second, to_later, to_first, to_taps], axis=0)


def matrices(table_ref):
    size = table_ref.shape[1]
    return [lambda at=slice(k * size, (k + 1) * size): table_ref[at, :] for k in range(5)]


def passed_along(block, distance):
    devices = range(lax.axis_size(CTX))
    route = [(i - distance, i) for i in devices if i - distance in devices]
    return lax.ppermute(block, CTX, route)


def wide(row_mask, columns):
    return jnp.concatenate([row_mask] * (columns // LANES), axis=1)


def row_ids(rows):
    return lax.broadcasted_iota(jnp.int32, (rows, LANES), 0)


def cuts_of(lengths_ref, rows):
    at = -lax.axis_index(CTX) * rows
    cuts = [at]
    for d in range(lengths_ref.shape[1]):
        at = at + lengths_ref[0, d]
        cuts.append(at)
    return cuts


def begin_at(cuts, at):
    begin = cuts[0]
    for cut in cuts[1:-1]:
        begin = jnp.where(cut <= at, cut, begin)
    return begin


def end_at(cuts, at):
    end = cuts[-1]
    for cut in cuts[-2:0:-1]:
        end = jnp.where(cut > at, cut, end)
    return end


def times(left, right, conjugate_left):
    half = left.shape[0] // 2
    a, b = left[:half], left[half:]
    c, d = right[:half], right[half:]
    if conjugate_left:
        return jnp.concatenate([a * c + b * d, a * d - b * c], axis=0)
    return jnp.concatenate([a * c - b * d, a * d + b * c], axis=0)


def dot(matrix, data):
    return jnp.dot(matrix, jnp.concatenate([data, data], axis=0), preferred_element_type=F32)


def back_dot(matrix, data):
    both = jnp.dot(matrix, data, preferred_element_type=F32)
    half = matrix.shape[0] // 2
    return both[:half] + both[half:]


def on_first_step(fill):
    pl.when(pl.program_id(0) == 0)(fill)


def mix_kernel(half_ref, lengths_ref, v_ref, before_ref, gs_ref, taps_ref, mixed_ref, short_ref, ext, reach_s):
    rows, columns = v_ref.shape

    @on_first_step
    def _():
        at = row_ids(rows)
        reach_s[...] = at - begin_at(cuts_of(lengths_ref, rows), at)

    ext[0:RIM, :] = before_ref[...].astype(F32)
    ext[RIM:, :] = v_ref[...].astype(F32)
    reach = wide(reach_s[...], columns)
    total = taps_ref[0:1, :] * ext[RIM:, :]
    for j in range(1, taps_ref.shape[0]):
        window = ext[RIM - j : RIM - j + rows, :]
        total = total + taps_ref[j : j + 1, :] * jnp.where(reach >= j, window, 0.0)
    short_ref[...] = total
    mixed_ref[...] = (gs_ref[...].astype(F32) * total).astype(BF)


def note_cuts(lengths_ref, rows, cuts_s):
    low, high = -1, -1
    cuts = cuts_of(lengths_ref, rows)
    for d, cut in enumerate(cuts):
        cuts_s[d] = cut
        if d < len(cuts) - 1:
            low = low + (cut <= 0).astype(jnp.int32)
            high = high + (cut <= rows - 1).astype(jnp.int32)
    return low, high


def own_kernel(half_ref, lengths_ref, mixed_ref, adj_ref, ltaps_ref, table_ref,
               back_ref, grads_ref, taps_spec, spec_acc, cuts_s):
    rows, columns = mixed_ref.shape
    first, second, _, front, totaps = matrices(table_ref)
    low, high = note_cuts(lengths_ref, rows, cuts_s)
    taps_spec[...] = dot(first(), ltaps_ref[...].astype(BF))
    at = row_ids(rows)

    def document(d, begun):
        inside = jnp.where((at >= cuts_s[d]) & (at < cuts_s[d + 1]), 1.0, 0.0)
        own_bf = wide(inside.astype(BF), columns)
        x_spec = dot(second(), mixed_ref[...] * own_bf)
        a_spec = dot(first(), adj_ref[...] * own_bf)
        terms = times(a_spec, x_spec, True)
        spec_acc[...] = spec_acc[...] + terms if begun else terms
        product = times(taps_spec[...], a_spec, True).astype(BF)
        back = wide(inside, columns) * back_dot(front(), product)
        back_ref[...] = back_ref[...] + back if begun else back
        return begun

    document(low, 0)
    lax.fori_loop(low + 1, high + 1, lambda d, carry: document(d, 1), 1)
    grads_ref[...] = back_dot(totaps(), spec_acc[...].astype(BF))


def grad_kernel(half_ref, lengths_ref, v_ref, before_ref, gs_ref, adj_ref, short_ref, back_ref, own_grads_ref,
                prev_ref, next_ref, staps_ref, ltaps_ref, table_ref, *rest):
    ggs_ref, adjs_ref, head_ref, grads_ref, ext, reach_s, masks_s = rest[-7:]
    rows, columns = v_ref.shape
    first, second, _, front, totaps = matrices(table_ref)

    @on_first_step
    def _():
        at = row_ids(rows)
        cuts = cuts_of(lengths_ref, rows)
        reach_s[...] = at - begin_at(cuts, at)
        ones = lambda mask: jnp.where(mask, 1.0, 0.0).astype(BF)
        masks_s[0 * rows : 1 * rows, :] = ones(at < end_at(cuts, 0))
        masks_s[1 * rows : 2 * rows, :] = ones(at - rows >= begin_at(cuts, 0))
        masks_s[2 * rows : 3 * rows, :] = ones(at >= begin_at(cuts, rows - 1))
        masks_s[3 * rows : 4 * rows, :] = ones(at + rows < end_at(cuts, rows - 1))

    mask = lambda k: wide(masks_s[k * rows : (k + 1) * rows, :], columns)
    taps_spec = dot(first(), ltaps_ref[...].astype(BF))
    next_spec = dot(second(), next_ref[...] * mask(3))
    product = times(taps_spec, next_spec, True).astype(BF)
    back = back_ref[...] + mask(2).astype(F32) * back_dot(front(), product)
    prev_spec = dot(first(), prev_ref[...] * mask(1))
    own_spec = dot(first(), adj_ref[...] * mask(0))
    product = times(own_spec, prev_spec, True).astype(BF)
    long_terms = own_grads_ref[...] + back_dot(totaps(), product)

    ggs_ref[...] = (back * short_ref[...]).astype(BF)
    adj_short = (back * gs_ref[...].astype(F32)).astype(BF)
    adjs_ref[...] = adj_short
    adj_short = adj_short.astype(F32)
    head_ref[...] = adj_short[0:RIM].astype(BF)
    ext[0:RIM, :] = before_ref[...].astype(F32)
    ext[RIM:, :] = v_ref[...].astype(F32)
    reach = wide(reach_s[...], columns)
    terms = [jnp.sum(adj_short * ext[RIM:, :], axis=0, keepdims=True)]
    for j in range(1, staps_ref.shape[0]):
        window = ext[RIM - j : RIM - j + rows, :]
        terms.append(jnp.sum(jnp.where(reach >= j, adj_short * window, 0.0), axis=0, keepdims=True))
    terms.append(jnp.zeros((RIM - len(terms), columns), F32))
    terms = jnp.concatenate([long_terms] + terms, axis=0).astype(BF)
    for k in range(columns // LANES):
        grads_ref[k] = terms[:, k * LANES : (k + 1) * LANES]


def long_kernel(half_ref, lengths_ref, gl_ref, up_ref, mixed_ref, prev_ref, ltaps_ref, table_ref, *rest):
    out_ref, ggl_ref, taps_spec, long_acc, cuts_s = rest[-5:]
    rows, columns = gl_ref.shape
    first, second, later, _, _ = matrices(table_ref)
    low, high = note_cuts(lengths_ref, rows, cuts_s)
    at = row_ids(rows)
    earlier = jnp.where(at - rows >= cuts_s[low], 1.0, 0.0).astype(BF)
    taps_spec[...] = dot(first(), ltaps_ref[...].astype(BF))

    def document(d, begun):
        inside = jnp.where((at >= cuts_s[d]) & (at < cuts_s[d + 1]), 1.0, 0.0)
        x_spec = dot(second(), mixed_ref[...] * wide(inside.astype(BF), columns))
        if not begun:
            x_spec = x_spec + dot(first(), prev_ref[...] * wide(earlier, columns))
        product = times(taps_spec[...], x_spec, False).astype(BF)
        mix = wide(inside, columns) * back_dot(later(), product)
        long_acc[...] = long_acc[...] + mix if begun else mix
        return begun

    document(low, 0)
    lax.fori_loop(low + 1, high + 1, lambda d, carry: document(d, 1), 1)
    long_mix = long_acc[...]
    out_ref[...] = (gl_ref[...].astype(F32) * long_mix).astype(BF)
    ggl_ref[...] = (up_ref[...].astype(F32) * long_mix).astype(BF)


def values_kernel(lengths_ref, adjs_ref, after_ref, taps_ref, gv_ref, move):
    rows, columns = adjs_ref.shape
    count = taps_ref.shape[0]

    @on_first_step
    def _():
        at = lax.broadcasted_iota(jnp.int32, (rows, 2 * LANES), 0)
        source = lax.broadcasted_iota(jnp.int32, (rows, 2 * LANES), 1)
        left = end_at(cuts_of(lengths_ref, rows), at) - at
        for j in range(count):
            move[j * rows : (j + 1) * rows, :] = jnp.where(
                (source == at + j) & (left > j), 1.0, 0.0).astype(BF)

    rim = jnp.concatenate([after_ref[...].astype(F32), jnp.zeros((LANES - RIM, columns), F32)], axis=0)
    data = jnp.concatenate([adjs_ref[...], rim.astype(BF)], axis=0)
    moved = jnp.dot(move[...], data, preferred_element_type=F32)
    total = taps_ref[0:1, :] * moved[:rows]
    for j in range(1, count):
        total = total + taps_ref[j : j + 1, :] * moved[j * rows : (j + 1) * rows]
    gv_ref[...] = total.astype(BF)


def spread_kernel(mine_ref, other_ref, short_ref, long_ref):
    rows = long_ref.shape[0]

    def write(blocks):
        for k in range(blocks.shape[0]):
            shares = blocks[k].astype(F32)
            at = slice(k * LANES, (k + 1) * LANES)
            long_ref[:, at] = shares[:rows]
            short_ref[:, at] = shares[rows : rows + short_ref.shape[0]]

    own_turn = pl.program_id(0) == lax.axis_index("core")
    pl.when(own_turn)(lambda: write(mine_ref))
    pl.when(jnp.logical_not(own_turn))(lambda: write(other_ref))


class Kernels:

    def __init__(self, rows, channels, count):
        self.rows, self.channels, self.count = rows, channels, count
        self.parts = channels // LANES
        self.table = jnp.asarray(spectra(rows))

    def call(self, kernel, step_parts, half, ins, outs, scratch, cost, mib, filled=()):
        columns = step_parts * LANES
        steps = self.parts // step_parts
        if half is not None:
            steps //= 2

        def spec(kind, shape):
            if kind == "scalars":
                return pl.BlockSpec(memory_space=pltpu.SMEM)
            if kind == "table":
                return pl.BlockSpec(shape, lambda i, *h: (0,) * len(shape))
            if kind == "shares":
                return pl.BlockSpec((step_parts,) + shape[1:], lambda i, *h: (i, 0, 0))
            if kind == "whole" and half is not None:
                return pl.BlockSpec((shape[0], columns), lambda i, h: (0, h[0] * steps + i))
            return pl.BlockSpec((shape[0], columns), lambda i, *h: (0, i))

        prefetch = 0 if half is None else 1
        arrays = ([] if half is None else [half]) + [a for _, a in ins] + list(filled)
        in_specs = [spec(k, a.shape) for k, a in ins] + [pl.BlockSpec(memory_space=pl.ANY)] * len(filled)
        return pl.pallas_call(
            kernel,
            grid_spec=pltpu.PrefetchScalarGridSpec(
                num_scalar_prefetch=prefetch,
                grid=(steps,),
                in_specs=in_specs,
                out_specs=[spec(k, o.shape) for k, o in outs],
                scratch_shapes=[pltpu.VMEM((r, c if c else columns), t) if r else t for r, c, t in scratch],
            ),
            out_shape=[o for _, o in outs],
            input_output_aliases={prefetch + len(ins) + k: k for k in range(len(filled))},
            compiler_params=pltpu.CompilerParams(vmem_limit_bytes=mib << 20),
            cost_estimate=pl.CostEstimate(
                flops=0, bytes_accessed=int(cost * 3.5e6), transcendentals=0),
        )(*arrays)

    def shaped(self, rows, kind):
        width = self.channels // 2 if kind == "half" else self.channels
        return lambda t: (kind, jax.ShapeDtypeStruct((rows, width), t))

    def small(self):
        return min(8, self.parts // 4)

    def mix(self, half, lengths, v, before, gs, staps, mib):
        out = self.shaped(self.rows, "half")
        return self.call(
            mix_kernel, self.small(), half,
            [("scalars", lengths), ("whole", v), ("whole", before), ("whole", gs), ("whole", staps)],
            [out(BF), out(F32)],
            [(self.rows + RIM, 0, F32), (self.rows, LANES, jnp.int32)], 3, mib)

    def own(self, half, lengths, mixed, adj, ltaps):
        out = self.shaped(self.rows, "half")
        spectrum = (2 * self.rows, 0, F32)
        return self.call(
            own_kernel, self.small(), half,
            [("scalars", lengths), ("half", mixed), ("whole", adj), ("whole", ltaps),
             ("table", self.table)],
            [out(F32)] * 2,
            [spectrum, spectrum, (0, 0, pltpu.SMEM((16,), jnp.int32))], 1.5, 28)

    def grad(self, half, lengths, v, before, gs, adj, short, back, own_grads, prev, following,
             staps, ltaps, filled):
        rows = self.rows
        out = self.shaped(rows, "whole")
        grads = jax.ShapeDtypeStruct((self.parts // 2, rows + RIM, LANES), BF)
        return self.call(
            grad_kernel, self.small(), half,
            [("scalars", lengths), ("whole", v), ("whole", before), ("whole", gs), ("whole", adj),
             ("half", short), ("half", back), ("half", own_grads), ("half", prev),
             ("whole", following), ("whole", staps), ("whole", ltaps), ("table", self.table)],
            [out(BF), out(BF), self.shaped(RIM, "whole")(BF), ("shares", grads)],
            [(rows + RIM, 0, F32), (rows, LANES, jnp.int32), (4 * rows, LANES, BF)], 1.5, 28, filled)

    def long(self, half, lengths, gl, up, mixed, prev, ltaps, filled):
        out = self.shaped(self.rows, "whole")
        spectrum = (2 * self.rows, 0, F32)
        return self.call(
            long_kernel, self.small(), half,
            [("scalars", lengths), ("whole", gl), ("whole", up), ("half", mixed), ("half", prev),
             ("whole", ltaps), ("table", self.table)],
            [out(BF)] * 2,
            [spectrum, (self.rows, 0, F32), (0, 0, pltpu.SMEM((16,), jnp.int32))], 3, 56, filled)

    def values_grad(self, lengths, adjs, after, staps):
        return self.call(
            values_kernel, 2 * self.small(), None,
            [("scalars", lengths), ("whole", adjs), ("whole", after), ("whole", staps)],
            [self.shaped(self.rows, "whole")(BF)],
            [(self.count * self.rows, 2 * LANES, BF)], 4, 56)[0]

    def spread(self, mine, other):
        return self.call(
            spread_kernel, self.parts // 2, None, [("table", mine), ("table", other)],
            [self.shaped(self.count, "whole")(F32), self.shaped(self.rows, "whole")(F32)], [], 3, 24)


def traded(block, axes):
    return lax.all_to_all(block, axes, 0, 0, tiled=True)


def copies(block, axes):
    return traded(jnp.broadcast_to(block[None], (lax.axis_size(axes),) + block.shape), axes)


def added(blocks):
    return jnp.sum(blocks.astype(F32), axis=0)


def swapped(block):
    return lax.ppermute(block, "core", [(0, 1), (1, 0)])


def on_device(lengths, values, gate_short, gate_long, short_taps, long_taps, cotangent):
    v, gs, gl, up = values[0], gate_short[0], gate_long[0], cotangent[0]
    rows, channels = v.shape
    k = Kernels(rows, channels, short_taps.shape[0])
    factor = 1.0 / math.sqrt(lax.axis_size(("y", "core", "z", "x")) * rows)
    together = lax.optimization_barrier

    core = lax.axis_index("core").astype(jnp.int32)
    kept = core[None]
    given = 1 - kept

    before = passed_along(v[rows - RIM :], 1)
    adj = (up.astype(F32) * gl.astype(F32)).astype(BF)
    before, adj = together((before, adj))
    following = passed_along(adj, -1)
    mixed_a, short_a = k.mix(given, lengths, v, before, gs, short_taps, 56)
    prev_a = passed_along(mixed_a, 1)
    back_a, terms_a = k.own(given, lengths, mixed_a, adj, long_taps)
    before, back_a = together((before, back_a))
    mixed_b, short_b = k.mix(kept, lengths, v, before, gs, short_taps, 20)
    prev_b = passed_along(mixed_b, 1)
    back_b, terms_b = k.own(kept, lengths, mixed_b, adj, long_taps)
    prev_a, back_b = together((prev_a, back_b))
    ggs, adjs, head, grads_a = k.grad(given, lengths, v, before, gs, adj, short_a, back_a, terms_a,
                                      prev_a, following, short_taps, long_taps, ())
    grads_a, prev_b = together((grads_a, prev_b))
    got = swapped(grads_a)
    ggs, adjs, head, grads_b = k.grad(kept, lengths, v, before, gs, adj, short_b, back_b, terms_b,
                                      prev_b, following, short_taps, long_taps, (ggs, adjs, head))

    planes = ("y", "x")
    half = (grads_b.astype(F32) + got.astype(F32)).astype(BF)
    half, mixed_a, mixed_b, head = together((half, mixed_a, mixed_b, head))
    share = half.reshape((lax.axis_size(planes), -1) + half.shape[1:])
    share = added(traded(share, planes)).astype(BF)
    after = passed_along(head, -1)
    filled = k.long(given, lengths, gl, up, mixed_a, prev_a, long_taps, ())
    share, after, filled, mixed_b = together((share, after, tuple(filled), mixed_b))
    share = (added(copies(share, "z")) * factor).astype(BF)
    out, ggl = k.long(kept, lengths, gl, up, mixed_b, prev_b, long_taps, filled)
    share, out, ggl, adjs = together((share, out, ggl, adjs))
    mine = copies(share, planes).reshape(half.shape)
    gv = k.values_grad(lengths, adjs, after, short_taps)
    mine, gv = together((mine, gv))
    grad_short, grad_long = k.spread(mine, swapped(mine))
    return out[None], ggs[None], gv[None], ggl[None], grad_short, grad_long


def solution(mesh):
    dp, ctx = mesh.shape["dp"], mesh.shape["ctx"]
    cut = jax.sharding.Mesh(mesh.devices.reshape(dp // 2, 2, ctx // 4, 4), ("y", "core", "z", "x"))
    rowed = P(("y", "core"), CTX, None)
    return jax.shard_map(
        on_device,
        mesh=cut,
        in_specs=(P(("y", "core"), None), rowed, rowed, rowed, P(), P(), rowed),
        out_specs=(rowed, rowed, rowed, rowed, P(), P()),
        check_vma=False,
    )
```

```python
import math

import jax
import jax.numpy as jnp
import numpy as np
from jax import lax
from jax.experimental import pallas as pl
from jax.experimental.pallas import tpu as pltpu
from jax.sharding import PartitionSpec as P

BF = jnp.bfloat16
F32 = jnp.float32
LANES = 128
RIM = 8
CTX = ("z", "x")


def halves(matrix):
    high = matrix.astype(np.float32).astype(BF)
    low = (matrix - high.astype(np.float64)).astype(np.float32).astype(BF)
    return high, low


def spectra(rows):
    points = 2 * rows
    theta = np.pi * (2 * np.arange(rows) + 1) / points
    angles = theta[:, None] * np.arange(points)[None, :]
    forward = np.concatenate([np.cos(angles), -np.sin(angles)], axis=0)
    inverse = forward.T / rows

    def pack(matrix):
        return np.concatenate(halves(matrix), axis=1)

    def stack(matrix):
        return np.concatenate(halves(matrix), axis=0)

    first = pack(forward[:, :rows])
    second = pack(forward[:, rows:])
    to_later = stack(inverse[rows:])
    to_first = stack(inverse[:rows])
    to_taps = stack(inverse[rows - np.arange(rows)])
    return np.concatenate([first, second, to_later, to_first, to_taps], axis=0)


def matrices(table_ref):
    size = table_ref.shape[1]
    return [lambda at=slice(k * size, (k + 1) * size): table_ref[at, :] for k in range(5)]


def passed_along(block, distance):
    devices = range(lax.axis_size(CTX))
    route = [(i - distance, i) for i in devices if i - distance in devices]
    return lax.ppermute(block, CTX, route)


def wide(row_mask, columns):
    return jnp.concatenate([row_mask] * (columns // LANES), axis=1)


def row_ids(rows):
    return lax.broadcasted_iota(jnp.int32, (rows, LANES), 0)


def cuts_of(lengths_ref, rows):
    at = -lax.axis_index(CTX) * rows
    cuts = [at]
    for d in range(lengths_ref.shape[1]):
        at = at + lengths_ref[0, d]
        cuts.append(at)
    return cuts


def begin_at(cuts, at):
    begin = cuts[0]
    for cut in cuts[1:-1]:
        begin = jnp.where(cut <= at, cut, begin)
    return begin


def end_at(cuts, at):
    end = cuts[-1]
    for cut in cuts[-2:0:-1]:
        end = jnp.where(cut > at, cut, end)
    return end


def times(left, right, conjugate_left):
    half = left.shape[0] // 2
    a, b = left[:half], left[half:]
    c, d = right[:half], right[half:]
    if conjugate_left:
        return jnp.concatenate([a * c + b * d, a * d - b * c], axis=0)
    return jnp.concatenate([a * c - b * d, a * d + b * c], axis=0)


def dot(matrix, data):
    return jnp.dot(matrix, jnp.concatenate([data, data], axis=0), preferred_element_type=F32)


def back_dot(matrix, data):
    both = jnp.dot(matrix, data, preferred_element_type=F32)
    half = matrix.shape[0] // 2
    return both[:half] + both[half:]


def on_first_step(fill):
    pl.when(pl.program_id(0) == 0)(fill)


def mix_kernel(half_ref, lengths_ref, v_ref, before_ref, gs_ref, taps_ref, mixed_ref, short_ref, ext, reach_s):
    rows, columns = v_ref.shape

    @on_first_step
    def _():
        at = row_ids(rows)
        reach_s[...] = at - begin_at(cuts_of(lengths_ref, rows), at)

    ext[0:RIM, :] = before_ref[...].astype(F32)
    ext[RIM:, :] = v_ref[...].astype(F32)
    reach = wide(reach_s[...], columns)
    total = taps_ref[0:1, :] * ext[RIM:, :]
    for j in range(1, taps_ref.shape[0]):
        window = ext[RIM - j : RIM - j + rows, :]
        total = total + taps_ref[j : j + 1, :] * jnp.where(reach >= j, window, 0.0)
    short_ref[...] = total
    mixed_ref[...] = (gs_ref[...].astype(F32) * total).astype(BF)


def note_cuts(lengths_ref, rows, cuts_s):
    low, high = -1, -1
    cuts = cuts_of(lengths_ref, rows)
    for d, cut in enumerate(cuts):
        cuts_s[d] = cut
        if d < len(cuts) - 1:
            low = low + (cut <= 0).astype(jnp.int32)
            high = high + (cut <= rows - 1).astype(jnp.int32)
    return low, high


def own_kernel(half_ref, lengths_ref, mixed_ref, adj_ref, ltaps_ref, table_ref,
               back_ref, grads_ref, taps_spec, spec_acc, cuts_s):
    rows, columns = mixed_ref.shape
    first, second, _, front, totaps = matrices(table_ref)
    low, high = note_cuts(lengths_ref, rows, cuts_s)
    taps_spec[...] = dot(first(), ltaps_ref[...].astype(BF))
    at = row_ids(rows)

    def document(d, begun):
        inside = jnp.where((at >= cuts_s[d]) & (at < cuts_s[d + 1]), 1.0, 0.0)
        own_bf = wide(inside.astype(BF), columns)
        x_spec = dot(second(), mixed_ref[...] * own_bf)
        a_spec = dot(first(), adj_ref[...] * own_bf)
        terms = times(a_spec, x_spec, True)
        spec_acc[...] = spec_acc[...] + terms if begun else terms
        product = times(taps_spec[...], a_spec, True).astype(BF)
        back = wide(inside, columns) * back_dot(front(), product)
        back_ref[...] = back_ref[...] + back if begun else back
        return begun

    document(low, 0)
    lax.fori_loop(low + 1, high + 1, lambda d, carry: document(d, 1), 1)
    grads_ref[...] = back_dot(totaps(), spec_acc[...].astype(BF))


def grad_kernel(half_ref, lengths_ref, v_ref, before_ref, gs_ref, adj_ref, short_ref, back_ref, own_grads_ref,
                prev_ref, next_ref, staps_ref, ltaps_ref, table_ref, *rest):
    ggs_ref, adjs_ref, head_ref, grads_ref, ext, reach_s, masks_s = rest[-7:]
    rows, columns = v_ref.shape
    first, second, _, front, totaps = matrices(table_ref)

    @on_first_step
    def _():
        at = row_ids(rows)
        cuts = cuts_of(lengths_ref, rows)
        reach_s[...] = at - begin_at(cuts, at)
        ones = lambda mask: jnp.where(mask, 1.0, 0.0).astype(BF)
        masks_s[0 * rows : 1 * rows, :] = ones(at < end_at(cuts, 0))
        masks_s[1 * rows : 2 * rows, :] = ones(at - rows >= begin_at(cuts, 0))
        masks_s[2 * rows : 3 * rows, :] = ones(at >= begin_at(cuts, rows - 1))
        masks_s[3 * rows : 4 * rows, :] = ones(at + rows < end_at(cuts, rows - 1))

    mask = lambda k: wide(masks_s[k * rows : (k + 1) * rows, :], columns)
    taps_spec = dot(first(), ltaps_ref[...].astype(BF))
    next_spec = dot(second(), next_ref[...] * mask(3))
    product = times(taps_spec, next_spec, True).astype(BF)
    back = back_ref[...] + mask(2).astype(F32) * back_dot(front(), product)
    prev_spec = dot(first(), prev_ref[...] * mask(1))
    own_spec = dot(first(), adj_ref[...] * mask(0))
    product = times(own_spec, prev_spec, True).astype(BF)
    long_terms = own_grads_ref[...] + back_dot(totaps(), product)

    ggs_ref[...] = (back * short_ref[...]).astype(BF)
    adj_short = (back * gs_ref[...].astype(F32)).astype(BF)
    adjs_ref[...] = adj_short
    adj_short = adj_short.astype(F32)
    head_ref[...] = adj_short[0:RIM].astype(BF)
    ext[0:RIM, :] = before_ref[...].astype(F32)
    ext[RIM:, :] = v_ref[...].astype(F32)
    reach = wide(reach_s[...], columns)
    terms = [jnp.sum(adj_short * ext[RIM:, :], axis=0, keepdims=True)]
    for j in range(1, staps_ref.shape[0]):
        window = ext[RIM - j : RIM - j + rows, :]
        terms.append(jnp.sum(jnp.where(reach >= j, adj_short * window, 0.0), axis=0, keepdims=True))
    terms.append(jnp.zeros((RIM - len(terms), columns), F32))
    terms = jnp.concatenate([long_terms] + terms, axis=0).astype(BF)
    for k in range(columns // LANES):
        grads_ref[k] = terms[:, k * LANES : (k + 1) * LANES]


def long_kernel(half_ref, lengths_ref, gl_ref, up_ref, mixed_ref, prev_ref, ltaps_ref, table_ref, *rest):
    out_ref, ggl_ref, taps_spec, long_acc, cuts_s = rest[-5:]
    rows, columns = gl_ref.shape
    first, second, later, _, _ = matrices(table_ref)
    low, high = note_cuts(lengths_ref, rows, cuts_s)
    at = row_ids(rows)
    earlier = jnp.where(at - rows >= cuts_s[low], 1.0, 0.0).astype(BF)
    taps_spec[...] = dot(first(), ltaps_ref[...].astype(BF))

    def document(d, begun):
        inside = jnp.where((at >= cuts_s[d]) & (at < cuts_s[d + 1]), 1.0, 0.0)
        x_spec = dot(second(), mixed_ref[...] * wide(inside.astype(BF), columns))
        if not begun:
            x_spec = x_spec + dot(first(), prev_ref[...] * wide(earlier, columns))
        product = times(taps_spec[...], x_spec, False).astype(BF)
        mix = wide(inside, columns) * back_dot(later(), product)
        long_acc[...] = long_acc[...] + mix if begun else mix
        return begun

    document(low, 0)
    lax.fori_loop(low + 1, high + 1, lambda d, carry: document(d, 1), 1)
    long_mix = long_acc[...]
    out_ref[...] = (gl_ref[...].astype(F32) * long_mix).astype(BF)
    ggl_ref[...] = (up_ref[...].astype(F32) * long_mix).astype(BF)


def values_kernel(lengths_ref, adjs_ref, after_ref, taps_ref, gv_ref, move):
    rows, columns = adjs_ref.shape
    count = taps_ref.shape[0]

    @on_first_step
    def _():
        at = lax.broadcasted_iota(jnp.int32, (rows, 2 * LANES), 0)
        source = lax.broadcasted_iota(jnp.int32, (rows, 2 * LANES), 1)
        left = end_at(cuts_of(lengths_ref, rows), at) - at
        for j in range(count):
            move[j * rows : (j + 1) * rows, :] = jnp.where(
                (source == at + j) & (left > j), 1.0, 0.0).astype(BF)

    rim = jnp.concatenate([after_ref[...].astype(F32), jnp.zeros((LANES - RIM, columns), F32)], axis=0)
    data = jnp.concatenate([adjs_ref[...], rim.astype(BF)], axis=0)
    moved = jnp.dot(move[...], data, preferred_element_type=F32)
    total = taps_ref[0:1, :] * moved[:rows]
    for j in range(1, count):
        total = total + taps_ref[j : j + 1, :] * moved[j * rows : (j + 1) * rows]
    gv_ref[...] = total.astype(BF)


def spread_kernel(mine_ref, other_ref, short_ref, long_ref):
    rows = long_ref.shape[0]

    def write(blocks):
        for k in range(blocks.shape[0]):
            shares = blocks[k].astype(F32)
            at = slice(k * LANES, (k + 1) * LANES)
            long_ref[:, at] = shares[:rows]
            short_ref[:, at] = shares[rows : rows + short_ref.shape[0]]

    own_turn = pl.program_id(0) == lax.axis_index("core")
    pl.when(own_turn)(lambda: write(mine_ref))
    pl.when(jnp.logical_not(own_turn))(lambda: write(other_ref))


class Kernels:

    def __init__(self, rows, channels, count):
        self.rows, self.channels, self.count = rows, channels, count
        self.parts = channels // LANES
        self.table = jnp.asarray(spectra(rows))

    def call(self, kernel, step_parts, half, ins, outs, scratch, cost, mib, filled=()):
        columns = step_parts * LANES
        steps = self.parts // step_parts
        if half is not None:
            steps //= 2

        def spec(kind, shape):
            if kind == "scalars":
                return pl.BlockSpec(memory_space=pltpu.SMEM)
            if kind == "table":
                return pl.BlockSpec(shape, lambda i, *h: (0,) * len(shape))
            if kind == "shares":
                return pl.BlockSpec((step_parts,) + shape[1:], lambda i, *h: (i, 0, 0))
            if kind == "whole" and half is not None:
                return pl.BlockSpec((shape[0], columns), lambda i, h: (0, h[0] * steps + i))
            return pl.BlockSpec((shape[0], columns), lambda i, *h: (0, i))

        prefetch = 0 if half is None else 1
        arrays = ([] if half is None else [half]) + [a for _, a in ins] + list(filled)
        in_specs = [spec(k, a.shape) for k, a in ins] + [pl.BlockSpec(memory_space=pl.ANY)] * len(filled)
        return pl.pallas_call(
            kernel,
            grid_spec=pltpu.PrefetchScalarGridSpec(
                num_scalar_prefetch=prefetch,
                grid=(steps,),
                in_specs=in_specs,
                out_specs=[spec(k, o.shape) for k, o in outs],
                scratch_shapes=[pltpu.VMEM((r, c if c else columns), t) if r else t for r, c, t in scratch],
            ),
            out_shape=[o for _, o in outs],
            input_output_aliases={prefetch + len(ins) + k: k for k in range(len(filled))},
            compiler_params=pltpu.CompilerParams(vmem_limit_bytes=mib << 20),
            cost_estimate=pl.CostEstimate(
                flops=0, bytes_accessed=int(cost * 3.5e6), transcendentals=0),
        )(*arrays)

    def shaped(self, rows, kind):
        width = self.channels // 2 if kind == "half" else self.channels
        return lambda t: (kind, jax.ShapeDtypeStruct((rows, width), t))

    def small(self):
        return min(8, self.parts // 4)

    def mix(self, half, lengths, v, before, gs, staps, mib):
        out = self.shaped(self.rows, "half")
        return self.call(
            mix_kernel, self.small(), half,
            [("scalars", lengths), ("whole", v), ("whole", before), ("whole", gs), ("whole", staps)],
            [out(BF), out(F32)],
            [(self.rows + RIM, 0, F32), (self.rows, LANES, jnp.int32)], 3, mib)

    def own(self, half, lengths, mixed, adj, ltaps):
        out = self.shaped(self.rows, "half")
        spectrum = (2 * self.rows, 0, F32)
        return self.call(
            own_kernel, 2 * self.small(), half,
            [("scalars", lengths), ("half", mixed), ("whole", adj), ("whole", ltaps),
             ("table", self.table)],
            [out(F32)] * 2,
            [spectrum, spectrum, (0, 0, pltpu.SMEM((16,), jnp.int32))], 1.5, 28)

    def grad(self, half, lengths, v, before, gs, adj, short, back, own_grads, prev, following,
             staps, ltaps, filled):
        rows = self.rows
        out = self.shaped(rows, "whole")
        grads = jax.ShapeDtypeStruct((self.parts // 2, rows + RIM, LANES), BF)
        return self.call(
            grad_kernel, self.small(), half,
            [("scalars", lengths), ("whole", v), ("whole", before), ("whole", gs), ("whole", adj),
             ("half", short), ("half", back), ("half", own_grads), ("half", prev),
             ("whole", following), ("whole", staps), ("whole", ltaps), ("table", self.table)],
            [out(BF), out(BF), self.shaped(RIM, "whole")(BF), ("shares", grads)],
            [(rows + RIM, 0, F32), (rows, LANES, jnp.int32), (4 * rows, LANES, BF)], 1.5, 28, filled)

    def long(self, half, lengths, gl, up, mixed, prev, ltaps, filled):
        out = self.shaped(self.rows, "whole")
        spectrum = (2 * self.rows, 0, F32)
        return self.call(
            long_kernel, self.small(), half,
            [("scalars", lengths), ("whole", gl), ("whole", up), ("half", mixed), ("half", prev),
             ("whole", ltaps), ("table", self.table)],
            [out(BF)] * 2,
            [spectrum, (self.rows, 0, F32), (0, 0, pltpu.SMEM((16,), jnp.int32))], 3, 56, filled)

    def values_grad(self, lengths, adjs, after, staps):
        return self.call(
            values_kernel, 2 * self.small(), None,
            [("scalars", lengths), ("whole", adjs), ("whole", after), ("whole", staps)],
            [self.shaped(self.rows, "whole")(BF)],
            [(self.count * self.rows, 2 * LANES, BF)], 4, 56)[0]

    def spread(self, mine, other):
        return self.call(
            spread_kernel, self.parts // 2, None, [("table", mine), ("table", other)],
            [self.shaped(self.count, "whole")(F32), self.shaped(self.rows, "whole")(F32)], [], 3, 24)


def traded(block, axes):
    return lax.all_to_all(block, axes, 0, 0, tiled=True)


def copies(block, axes):
    return traded(jnp.broadcast_to(block[None], (lax.axis_size(axes),) + block.shape), axes)


def added(blocks):
    return jnp.sum(blocks.astype(F32), axis=0)


def swapped(block):
    return lax.ppermute(block, "core", [(0, 1), (1, 0)])


def on_device(lengths, values, gate_short, gate_long, short_taps, long_taps, cotangent):
    v, gs, gl, up = values[0], gate_short[0], gate_long[0], cotangent[0]
    rows, channels = v.shape
    k = Kernels(rows, channels, short_taps.shape[0])
    factor = 1.0 / math.sqrt(lax.axis_size(("y", "core", "z", "x")) * rows)
    together = lax.optimization_barrier

    core = lax.axis_index("core").astype(jnp.int32)
    kept = core[None]
    given = 1 - kept

    before = passed_along(v[rows - RIM :], 1)
    adj = (up.astype(F32) * gl.astype(F32)).astype(BF)
    before, adj = together((before, adj))
    following = passed_along(adj, -1)
    mixed_a, short_a = k.mix(given, lengths, v, before, gs, short_taps, 56)
    prev_a = passed_along(mixed_a, 1)
    back_a, terms_a = k.own(given, lengths, mixed_a, adj, long_taps)
    before, back_a = together((before, back_a))
    mixed_b, short_b = k.mix(kept, lengths, v, before, gs, short_taps, 20)
    prev_b = passed_along(mixed_b, 1)
    back_b, terms_b = k.own(kept, lengths, mixed_b, adj, long_taps)
    prev_a, back_b = together((prev_a, back_b))
    ggs, adjs, head, grads_a = k.grad(given, lengths, v, before, gs, adj, short_a, back_a, terms_a,
                                      prev_a, following, short_taps, long_taps, ())
    grads_a, prev_b = together((grads_a, prev_b))
    got = swapped(grads_a)
    ggs, adjs, head, grads_b = k.grad(kept, lengths, v, before, gs, adj, short_b, back_b, terms_b,
                                      prev_b, following, short_taps, long_taps, (ggs, adjs, head))

    planes = ("y", "x")
    half = (grads_b.astype(F32) + got.astype(F32)).astype(BF)
    half, mixed_a, mixed_b, head = together((half, mixed_a, mixed_b, head))
    share = half.reshape((lax.axis_size(planes), -1) + half.shape[1:])
    share = added(traded(share, planes)).astype(BF)
    after = passed_along(head, -1)
    filled = k.long(given, lengths, gl, up, mixed_a, prev_a, long_taps, ())
    share, after, filled, mixed_b = together((share, after, tuple(filled), mixed_b))
    share = (added(copies(share, "z")) * factor).astype(BF)
    out, ggl = k.long(kept, lengths, gl, up, mixed_b, prev_b, long_taps, filled)
    share, out, ggl, adjs = together((share, out, ggl, adjs))
    mine = copies(share, planes).reshape(half.shape)
    gv = k.values_grad(lengths, adjs, after, short_taps)
    mine, gv = together((mine, gv))
    grad_short, grad_long = k.spread(mine, swapped(mine))
    return out[None], ggs[None], gv[None], ggl[None], grad_short, grad_long


def solution(mesh):
    dp, ctx = mesh.shape["dp"], mesh.shape["ctx"]
    cut = jax.sharding.Mesh(mesh.devices.reshape(dp // 2, 2, ctx // 4, 4), ("y", "core", "z", "x"))
    rowed = P(("y", "core"), CTX, None)
    return jax.shard_map(
        on_device,
        mesh=cut,
        in_specs=(P(("y", "core"), None), rowed, rowed, rowed, P(), P(), rowed),
        out_specs=(rowed, rowed, rowed, rowed, P(), P()),
        check_vma=False,
    )
```
